512 devices in a mesh: gx: 32 (over z, x), gy: 16 (over y, core).
Axes of the slice: x: 4, y: 8, z: 8, core: 2. Of those that a mesh axis runs over, the one named last changes fastest.
Arguments:
- density: float32 [4, 128, 256, 128], P(None, 'gx', 'gy'), may hold values from 0 to 12, as said below
- rate_table: float32 [4, 9], replicated, may hold values from 0 to 128, as said below
Outputs:
- propagated: float32 [4, 128, 256, 128], P(None, 'gx', 'gy')
- step_entries: float32 [4, 5], replicated
The draws below stay inside these ranges and needn't reach their ends.
Inputs may be any that keep to these rules, and one draw needn't show every extreme that they name: `density`: every entry is positive. `rate_table`: all entries positive; entry r of a row is the constant cr of the steps.
All inputs are finite; a program needn't handle non-finite values.
Results may differ from the reference program's by a relative error of at most 0.0006.
Values sent between devices are 32-bit elements; how exact they have to be, the bound alone decides.
A program may use at most 64 MiB of HBM per device.

```python
import jax
import jax.numpy as jnp
from jax import lax

CI = 4
NK = 128
MEMBERS = 4
NI = 128
NJ = 256
N_GX = 32


def draw_density(key, part):
    full_shape = (MEMBERS, NI, NJ, NK)
    place_i = (jnp.arange(NI, dtype=jnp.float32) / NI)[:, None, None]
    place_j = (jnp.arange(NJ, dtype=jnp.float32) / NJ)[None, :, None]
    roughness = jnp.exp(jax.random.uniform(key, full_shape, jnp.float32, -0.6931, 0.6931))
    profile = jnp.power(10.0, place_i - 0.5) * jnp.power(3.0, place_j - 0.5)
    return roughness * profile[None]


def draw_rate_table(key, part):
    base_rates = jnp.array([40.0, 25.0 / NI, 40.0, 30.0 / NJ, 52.0 / (NI * NI), 13.0 / NK, 13.0 / NK, NJ / 4.0, NK / 4.0], dtype=jnp.float32)
    factor = jnp.exp(jax.random.uniform(key, (MEMBERS, 9), jnp.float32, -0.6931, 0.6931))
    return base_rates[None, :] * factor


def setup_inputs(seed: int = 0) -> dict:
    splits = jax.random.split(jax.random.key(seed), 3)
    density = draw_density(jax.random.fold_in(splits[2], 71), 0)
    rate_table = draw_rate_table(jax.random.fold_in(splits[2], 71), 0)
    return dict(density=density, rate_table=rate_table)


tau_step = 0.01
taylor_terms = 16
squarings = 4

def shift_down(vector_field):
    return jnp.concatenate([jnp.zeros_like(vector_field[..., :1]), vector_field[..., :-1]], axis=-1)

def shift_up(vector_field):
    return jnp.concatenate([vector_field[..., 1:], jnp.zeros_like(vector_field[..., :1])], axis=-1)

def generator_apply(padded, first_i, first_j, member_rates):
    row_count = padded.shape[0] - 4
    col_count = padded.shape[1] - 2
    lattice_depth = padded.shape[2]
    amount_i = (first_i + jnp.arange(row_count, dtype=jnp.int32)).astype(jnp.float32)[:, None, None]
    amount_j = (first_j + jnp.arange(col_count, dtype=jnp.int32)).astype(jnp.float32)[None, :, None]
    amount_k = jnp.arange(lattice_depth, dtype=jnp.int32).astype(jnp.float32)[None, None, :]
    ratio_j = amount_j / member_rates[7]
    ratio_k = amount_k / member_rates[8]
    make_u = member_rates[0] / (1.0 + ratio_j * ratio_j)
    make_v = member_rates[2] / (1.0 + ratio_k * ratio_k)
    outflow = make_u + member_rates[1] * amount_i + make_v + member_rates[3] * amount_j
    outflow = outflow + 0.5 * member_rates[4] * amount_i * (amount_i - 1.0) + (member_rates[5] + member_rates[6]) * amount_k
    centre = padded[2:-2, 1:-1]
    inflow = make_u * padded[1:-3, 1:-1]
    inflow = inflow + member_rates[1] * (amount_i + 1.0) * padded[3:-1, 1:-1]
    inflow = inflow + make_v * padded[2:-2, :-2]
    inflow = inflow + member_rates[3] * (amount_j + 1.0) * padded[2:-2, 2:]
    inflow = inflow + 0.5 * member_rates[4] * (amount_i + 2.0) * (amount_i + 1.0) * shift_down(padded[4:, 1:-1])
    inflow = inflow + member_rates[5] * (amount_k + 1.0) * shift_up(padded[:-4, 1:-1])
    inflow = inflow + member_rates[6] * (amount_k + 1.0) * shift_up(centre)
    return inflow - outflow * centre

def matrix_exponential(small):
    scaled = small * (tau_step / 2.0 ** squarings)
    identity = jnp.eye(3, dtype=jnp.float32)
    series = identity + jnp.zeros_like(scaled)
    for term_index in range(taylor_terms, 0, -1):
        series = identity + jnp.einsum('...ab,...bc->...ac', scaled, series, precision=lax.Precision.HIGHEST) / term_index
    for square_index in range(squarings):
        series = jnp.einsum('...ab,...bc->...ac', series, series, precision=lax.Precision.HIGHEST)
    return series

def apply_member(vector_field, member_rates):
    padded_full = jnp.pad(vector_field, ((2, 2), (1, 1), (0, 0)))
    starts = jnp.arange(N_GX, dtype=jnp.int32) * CI

    def one_block(block_start):
        slab_rows = lax.dynamic_slice_in_dim(padded_full, block_start, CI + 4, 0)
        return generator_apply(slab_rows, block_start, jnp.int32(0), member_rates)
    return lax.map(one_block, starts).reshape(vector_field.shape)

def one_member(pair):
    field_one, member_rates = pair
    basis_scale = jnp.sqrt(jnp.sum(field_one * field_one))
    basis_zero = field_one / basis_scale
    candidate = apply_member(basis_zero, member_rates)
    entry_00 = jnp.sum(basis_zero * candidate)
    candidate = candidate - entry_00 * basis_zero
    entry_10 = jnp.sqrt(jnp.sum(candidate * candidate))
    basis_one = candidate / entry_10
    candidate = apply_member(basis_one, member_rates)
    entry_01 = jnp.sum(basis_zero * candidate)
    entry_11 = jnp.sum(basis_one * candidate)
    candidate = candidate - entry_01 * basis_zero - entry_11 * basis_one
    entry_21 = jnp.sqrt(jnp.sum(candidate * candidate))
    basis_two = candidate / entry_21
    zeros = jnp.zeros_like(entry_00)
    small = jnp.stack([jnp.stack([entry_00, entry_01, zeros], -1), jnp.stack([entry_10, entry_11, zeros], -1), jnp.stack([zeros, entry_21, zeros], -1)], -2)
    propagator = matrix_exponential(small)
    propagated = basis_scale * (propagator[0, 0] * basis_zero + propagator[1, 0] * basis_one + propagator[2, 0] * basis_two)
    entries = tau_step * jnp.stack([entry_00, entry_10, entry_01, entry_11, entry_21], -1)
    return (propagated, entries)

def reference(density, rate_table):
    propagated_all, entries_all = lax.map(one_member, (density, rate_table))
    return (propagated_all, entries_all)
```

```python
import functools
import itertools

import jax
import jax.numpy as jnp
from jax import lax
from jax.experimental import pallas as pl
from jax.experimental.pallas import tpu as pltpu
from jax.sharding import PartitionSpec as P

MESH = pl.DeviceIdType.MESH
F32 = jnp.float32
TAU = 0.01
TAYLOR_TERMS = 16
SQUARINGS = 4
M, CI, CJ, NK = 4, 4, 16, 128
NI, NJ = 128, 256
GX, GY = 32, 16
PAIRS = ((0, 0), (0, 1), (0, 2), (1, 1), (1, 2), (2, 2))


def ring(size):
    return sorted(range(1, size), key=lambda a: -min(a, size - a))


def hops_gx(a):
    z, x = a // 4, a % 4
    return min(z, 8 - z) + min(x, 4 - x)


STAGE_GX = sorted(range(1, GX), key=lambda a: -hops_gx(a))
STAGE_GY = ring(GY)


def roll_lanes(value, shift):
    return pltpu.roll(value, shift % NK, value.ndim - 1)


def kernel(
    d_ref, rate_ref, out_ref, entry_ref,
    dpad, upad, from_lo, from_hi, col_out, col_in, cor_out, cor_in, strip,
    rows, total, slots_gx, slots_gy,
    x_send, x_recv, y_send, y_recv, c_send, c_recv, r_send, r_recv,
):
    gx, gy = lax.axis_index("gx"), lax.axis_index("gy")
    first_i, first_j = gx * CI, gy * CJ
    has_x = (gx > 0, gx < GX - 1)
    has_y = (gy > 0, gy < GY - 1)
    step = (-1, 1)

    def at(dx, dy):
        return (gx + dx, gy + dy)

    barrier = pltpu.get_barrier_semaphore()
    for a in STAGE_GX:
        pl.semaphore_signal(barrier, inc=1, device_id=(lax.rem(gx + a, GX), gy), device_id_type=MESH)
    for a in STAGE_GY:
        pl.semaphore_signal(barrier, inc=1, device_id=(gx, lax.rem(gy + a, GY)), device_id_type=MESH)
    for sx, sy in itertools.product((0, 1), (0, 1)):
        @pl.when(has_x[sx] & has_y[sy])
        def _(sx=sx, sy=sy):
            pl.semaphore_signal(barrier, inc=1, device_id=at(step[sx], step[sy]), device_id_type=MESH)

    for sy, (near, far) in enumerate(((0, 1), (CJ - 1, CJ - 2))):
        for m in range(M):
            for r in range(CI):
                col_out[sy, m, r : r + 1] = d_ref[m, r, near : near + 1]
                col_out[sy, m, CI + r : CI + r + 1] = d_ref[m, r, far : far + 1]
            for sx, r0 in enumerate((0, CI - 2)):
                for q in range(2):
                    cor_out[sx, sy, 2 * m + q : 2 * m + q + 1] = d_ref[m, r0 + q, near : near + 1]

    n_x = (gx > 0).astype(jnp.int32) + (gx < GX - 1).astype(jnp.int32)
    n_y = (gy > 0).astype(jnp.int32) + (gy < GY - 1).astype(jnp.int32)
    pl.semaphore_wait(barrier, GX - 1 + GY - 1 + n_x * n_y)

    def x_copy(sx, m):
        dst = (from_hi, from_lo)[sx]
        return pltpu.make_async_remote_copy(
            src_ref=d_ref.at[m], dst_ref=dst.at[m], send_sem=x_send.at[sx, m], recv_sem=x_recv.at[1 - sx, m],
            device_id=at(step[sx], 0), device_id_type=MESH,
        )

    def y_copy(sy):
        return pltpu.make_async_remote_copy(
            src_ref=col_out.at[sy], dst_ref=col_in.at[1 - sy], send_sem=y_send.at[sy], recv_sem=y_recv.at[1 - sy],
            device_id=at(0, step[sy]), device_id_type=MESH,
        )

    def c_copy(sx, sy):
        return pltpu.make_async_remote_copy(
            src_ref=cor_out.at[sx, sy], dst_ref=cor_in.at[1 - sx, 1 - sy],
            send_sem=c_send.at[sx, sy], recv_sem=c_recv.at[1 - sx, 1 - sy],
            device_id=at(step[sx], step[sy]), device_id_type=MESH,
        )

    def incoming_x(sx, m):
        dst = (from_lo, from_hi)[sx]
        return pltpu.make_async_remote_copy(
            src_ref=d_ref.at[m], dst_ref=dst.at[m], send_sem=x_send.at[sx, m], recv_sem=x_recv.at[sx, m],
            device_id=at(step[sx], 0), device_id_type=MESH,
        )

    def incoming_y(sy):
        return pltpu.make_async_remote_copy(
            src_ref=col_out.at[sy], dst_ref=col_in.at[sy], send_sem=y_send.at[sy], recv_sem=y_recv.at[sy],
            device_id=at(0, step[sy]), device_id_type=MESH,
        )

    def incoming_c(sx, sy):
        return pltpu.make_async_remote_copy(
            src_ref=cor_out.at[sx, sy], dst_ref=cor_in.at[sx, sy],
            send_sem=c_send.at[sx, sy], recv_sem=c_recv.at[sx, sy],
            device_id=at(step[sx], step[sy]), device_id_type=MESH,
        )

    for sy in range(2):
        @pl.when(has_y[sy])
        def _(sy=sy):
            y_copy(sy).start()
    for sx, sy in itertools.product((0, 1), (0, 1)):
        @pl.when(has_x[sx] & has_y[sy])
        def _(sx=sx, sy=sy):
            c_copy(sx, sy).start()
    for m in range(M):
        for sx in range(2):
            @pl.when(has_x[sx])
            def _(sx=sx, m=m):
                x_copy(sx, m).start()

    lane = lax.broadcasted_iota(jnp.int32, (1, NK), 1)
    k_row = lane.astype(F32)
    not_first = (lane > 0).astype(F32)
    j_col = (first_j + lax.broadcasted_iota(jnp.int32, (CJ, NK), 0)).astype(F32)
    lam_row = jnp.ones((1, NK), F32)
    rates = []
    for m in range(M):
        c = [rate_ref[m, r] for r in range(9)]
        lam = c[0] + 127.0 * c[1] + c[2] + 255.0 * c[3] + 8001.0 * c[4] + 127.0 * (c[5] + c[6])
        lam_row = jnp.where(lane == m, lam, lam_row)
        rates.append(c)
    inv_row = 1.0 / lam_row

    def coefficients(m):
        inv = inv_row[0, m]
        c = [rates[m][r] * inv for r in range(7)] + rates[m][7:]
        ratio_j = j_col / c[7]
        ratio_k = k_row / c[8]
        make_u = c[0] / (1.0 + ratio_j * ratio_j)
        make_v = c[2] / (1.0 + ratio_k * ratio_k)
        gain_j = c[3] * (j_col + 1.0)
        loss = make_u + make_v + c[3] * j_col + (c[5] + c[6]) * k_row
        return c, make_u, make_v, gain_j, loss

    def row_scalars(c, r):
        i = (first_i + r).astype(F32)
        down = c[1] * (i + 1.0)
        pair = 0.5 * c[4] * (i + 2.0) * (i + 1.0)
        out = c[1] * i + 0.5 * c[4] * i * (i - 1.0)
        return down, pair, out

    def image(c, make_u, make_v, gain_j, loss, scalars, before2, before, here, after, after2, left, right):
        down, pair, out = scalars
        result = make_u * before + down * after + make_v * left + gain_j * right
        result = result + roll_lanes(after2, 1) * (pair * not_first)
        result = result + roll_lanes((c[5] * before2 + c[6] * here) * k_row, -1)
        return result - (loss + out) * here

    for sx in range(2):
        @pl.when(jnp.logical_not(has_x[sx]))
        def _(sx=sx):
            (from_lo, from_hi)[sx][...] = jnp.zeros_like(from_lo)
    for sy in range(2):
        @pl.when(jnp.logical_not(has_y[sy]))
        def _(sy=sy):
            col_in[sy] = jnp.zeros_like(col_in[sy])
    for sx, sy in itertools.product((0, 1), (0, 1)):
        @pl.when(jnp.logical_not(has_x[sx] & has_y[sy]))
        def _(sx=sx, sy=sy):
            cor_in[sx, sy] = jnp.zeros_like(cor_in[sx, sy])

    for m in range(M):
        for r in range(CI):
            dpad[m, r + 2, 8 : 8 + CJ] = d_ref[m, r]

    for sy in range(2):
        @pl.when(has_y[sy])
        def _(sy=sy):
            incoming_y(sy).wait_recv()
    for sx, sy in itertools.product((0, 1), (0, 1)):
        @pl.when(has_x[sx] & has_y[sy])
        def _(sx=sx, sy=sy):
            incoming_c(sx, sy).wait_recv()

    for m in range(M):
        for sy, at_col in enumerate((7, 8 + CJ)):
            for r in range(CI):
                dpad[m, r + 2, at_col : at_col + 1] = col_in[sy, m, r : r + 1]
            strip[m, sy, 2 : 2 + CI] = col_in[sy, m, 0:CI]
            for sx, r0 in enumerate((0, CI + 2)):
                strip[m, sy, r0 : r0 + 2] = cor_in[sx, sy, 2 * m : 2 * m + 2]
                for q in range(2):
                    dpad[m, r0 + q, at_col : at_col + 1] = cor_in[sx, sy, 2 * m + q : 2 * m + q + 1]

    inside_hi = (gx < GX - 1).astype(F32)
    for m in range(M):
        c, make_u, make_v, gain_j, loss = coefficients(m)
        for sx in range(2):
            @pl.when(has_x[sx])
            def _(sx=sx, m=m):
                incoming_x(sx, m).wait_recv()
        for q in range(2):
            dpad[m, q, 8 : 8 + CJ] = from_lo[m, 2 + q]
            dpad[m, CI + 2 + q, 8 : 8 + CJ] = from_hi[m, q]

        def full(r):
            if r < 0:
                return from_lo[m, CI + r]
            if r >= CI:
                return from_hi[m, r - CI]
            return d_ref[m, r]

        for r in range(-2, CI + 2):
            u = image(
                c, make_u, make_v, gain_j, loss, row_scalars(c, r),
                full(r - 2), full(r - 1), full(r), full(r + 1), full(r + 2),
                dpad[m, r + 2, 7 : 7 + CJ], dpad[m, r + 2, 9 : 9 + CJ],
            )
            if r >= CI:
                u = u * inside_hi
            upad[m, r + 2, 8 : 8 + CJ] = u

        i4 = (first_i + lax.broadcasted_iota(jnp.int32, (CI, NK), 0)).astype(F32)
        scalars = (
            c[1] * (i4 + 1.0),
            0.5 * c[4] * (i4 + 2.0) * (i4 + 1.0),
            c[1] * i4 + 0.5 * c[4] * i4 * (i4 - 1.0),
        )
        for sy, (jj, at_col) in enumerate(((-1, 7), (CJ, 8 + CJ))):
            j = jnp.full((1, NK), (first_j + jj).astype(F32))
            ratio = j / c[7]
            mu = c[0] / (1.0 + ratio * ratio)
            lo = mu + make_v + c[3] * j + (c[5] + c[6]) * k_row
            inner, outer = col_out[sy, m, 0:CI], col_in[sy, m, CI : 2 * CI]
            left, right = (outer, inner) if sy == 0 else (inner, outer)
            u = image(
                c, mu, make_v, c[3] * (j + 1.0), lo, scalars,
                strip[m, sy, 0:4], strip[m, sy, 1:5], strip[m, sy, 2:6], strip[m, sy, 3:7], strip[m, sy, 4:8],
                left, right,
            )
            if sy == 1:
                u = u * (gy < GY - 1).astype(F32)
            for r in range(CI):
                upad[m, r + 2, at_col : at_col + 1] = u[r : r + 1]

        sums = [jnp.zeros((8, NK), F32) for _ in PAIRS]
        for r in range(CI):
            mid = lambda q: upad[m, q + 2, 8 : 8 + CJ]
            u2 = image(
                c, make_u, make_v, gain_j, loss, row_scalars(c, r),
                mid(r - 2), mid(r - 1), mid(r), mid(r + 1), mid(r + 2),
                upad[m, r + 2, 7 : 7 + CJ], upad[m, r + 2, 9 : 9 + CJ],
            )
            out_ref[m, r] = u2
            basis = (d_ref[m, r], mid(r), u2)
            for p, (a, b) in enumerate(PAIRS):
                product = basis[a] * basis[b]
                sums[p] = sums[p] + product[0:8] + product[8:16]
        for p in range(len(PAIRS)):
            rows[p * M + m : p * M + m + 1] = jnp.sum(sums[p], axis=0, keepdims=True)

    n_rows = len(PAIRS) * M
    column = jnp.sum(rows[...], axis=1, keepdims=True)
    lanes = lax.broadcasted_iota(jnp.int32, (n_rows, NK), 1)
    places = lax.broadcasted_iota(jnp.int32, (n_rows, NK), 0)
    acc = jnp.sum(jnp.where(lanes == places, column, 0.0), axis=0, keepdims=True)

    for stage, (offsets, slots) in enumerate(((STAGE_GX, slots_gx), (STAGE_GY, slots_gy))):
        total[stage] = acc
        for a in offsets:
            peer = (lax.rem(gx + a, GX), gy) if stage == 0 else (gx, lax.rem(gy + a, GY))
            pltpu.make_async_remote_copy(
                src_ref=total.at[stage], dst_ref=slots.at[a - 1], send_sem=r_send.at[stage], recv_sem=r_recv.at[stage],
                device_id=peer, device_id_type=MESH,
            ).start()
        whole = pltpu.make_async_remote_copy(
            src_ref=slots, dst_ref=slots, send_sem=r_send.at[stage], recv_sem=r_recv.at[stage],
            device_id=(lax.rem(gx + 1, GX), gy), device_id_type=MESH,
        )
        whole.wait_recv()
        acc = acc + jnp.sum(slots[...], axis=0)
        whole.wait_send()

    picked = [acc if p == 0 else roll_lanes(acc, -M * p) for p in range(len(PAIRS))]
    ok = lane < M
    picked = [jnp.where(ok, value, 1.0) for value in picked]
    scale = 1.0 / picked[0]
    a1, a2, b11, b12, b22 = [value * scale for value in picked[1:]]
    h00 = a1
    n1 = b11 - h00 * h00
    h10 = jnp.sqrt(n1)
    e = a2 - h00 * a1
    h01 = e / h10
    h11 = ((b12 - h00 * b11) - h00 * e) / n1
    ss = (b22 - h00 * b12) - h00 * (b12 - h00 * b11)
    h21 = jnp.sqrt(ss / n1 - h01 * h01 - h11 * h11)

    step_scale = lam_row * TAU
    entries = [step_scale * h for h in (h00, h10, h01, h11, h21)]
    small = 1.0 / 2.0**SQUARINGS
    g00, g10, g01, g11, g21 = [entry * small for entry in entries]
    one, zero = jnp.ones_like(h00), jnp.zeros_like(h00)
    p00, p01, p10, p11 = one, zero, zero, one
    w0 = w1 = zero
    for term in range(TAYLOR_TERMS, 0, -1):
        f = 1.0 / term
        w0, w1 = g21 * f * p10, g21 * f * p11
        q00 = 1.0 + (g00 * f * p00 + g01 * f * p10)
        q01 = g00 * f * p01 + g01 * f * p11
        q10 = g10 * f * p00 + g11 * f * p10
        q11 = 1.0 + (g10 * f * p01 + g11 * f * p11)
        p00, p01, p10, p11 = q00, q01, q10, q11
    for _ in range(SQUARINGS):
        w0, w1 = w0 + (w0 * p00 + w1 * p10), w1 + (w0 * p01 + w1 * p11)
        q00 = p00 * p00 + p01 * p10
        q01 = p00 * p01 + p01 * p11
        q10 = p10 * p00 + p11 * p10
        q11 = p10 * p01 + p11 * p11
        p00, p01, p10, p11 = q00, q01, q10, q11
    e0, e1, e2 = p00, p10, w0
    inv10 = 1.0 / h10
    e2 = e2 / h21
    f0 = e0 - e1 * h00 * inv10 + e2 * (h11 * h00 * inv10 - h01)
    f1 = (e1 - e2 * (h00 + h11)) * inv10
    f2 = e2 * inv10

    eye = lax.broadcasted_iota(jnp.int32, (8, NK), 0) == lax.broadcasted_iota(jnp.int32, (8, NK), 1)
    lanes8 = lax.broadcasted_iota(jnp.int32, (8, NK), 1)
    table = jnp.zeros((8, NK), F32)
    for q, entry in enumerate(entries):
        column = jnp.sum(jnp.where(eye, entry, 0.0), axis=1, keepdims=True)
        table = jnp.where(lanes8 == q, column, table)
    entry_ref[...] = table[:M, :5]

    for m in range(M):
        s0, s1, s2 = (jnp.broadcast_to(f[:, m : m + 1], (CJ, NK)) for f in (f0, f1, f2))
        for r in range(CI):
            out_ref[m, r] = s0 * d_ref[m, r] + s1 * upad[m, r + 2, 8 : 8 + CJ] + s2 * out_ref[m, r]

    for sy in range(2):
        @pl.when(has_y[sy])
        def _(sy=sy):
            y_copy(sy).wait_send()
    for sx, sy in itertools.product((0, 1), (0, 1)):
        @pl.when(has_x[sx] & has_y[sy])
        def _(sx=sx, sy=sy):
            c_copy(sx, sy).wait_send()
    for m in range(M):
        for sx in range(2):
            @pl.when(has_x[sx])
            def _(sx=sx, m=m):
                x_copy(sx, m).wait_send()


def shards(density, rate_table):
    vmem = functools.partial(pltpu.VMEM, dtype=F32)
    dma = pltpu.SemaphoreType.DMA
    return pl.pallas_call(
        kernel,
        out_shape=(jax.ShapeDtypeStruct(density.shape, F32), jax.ShapeDtypeStruct((M, 5), F32)),
        in_specs=[pl.BlockSpec(memory_space=pltpu.VMEM), pl.BlockSpec(memory_space=pltpu.SMEM)],
        out_specs=(pl.BlockSpec(memory_space=pltpu.VMEM), pl.BlockSpec(memory_space=pltpu.VMEM)),
        scratch_shapes=[
            vmem((M, CI + 4, 32, NK)),
            vmem((M, CI + 4, 32, NK)),
            vmem((M, CI, CJ, NK)),
            vmem((M, CI, CJ, NK)),
            vmem((2, M, 8, NK)),
            vmem((2, M, 8, NK)),
            vmem((2, 2, 8, NK)),
            vmem((2, 2, 8, NK)),
            vmem((M, 2, 8, NK)),
            vmem((len(PAIRS) * M, NK)),
            vmem((2, 1, NK)),
            vmem((GX - 1, 1, NK)),
            vmem((GY - 1, 1, NK)),
            dma((2, M)),
            dma((2, M)),
            dma((2,)),
            dma((2,)),
            dma((2, 2)),
            dma((2, 2)),
            dma((2,)),
            dma((2,)),
        ],
        compiler_params=pltpu.CompilerParams(collective_id=0, has_side_effects=True),
    )(density, rate_table)


def solution(mesh):
    specs = (P(None, "gx", "gy", None), P())
    return jax.shard_map(shards, mesh=mesh, in_specs=specs, out_specs=specs, check_vma=False)
```

```python
import functools
import itertools

import jax
import jax.numpy as jnp
from jax import lax
from jax.experimental import pallas as pl
from jax.experimental.pallas import tpu as pltpu
from jax.sharding import PartitionSpec as P

MESH = pl.DeviceIdType.MESH
F32 = jnp.float32
TAU = 0.01
TAYLOR_TERMS = 16
SQUARINGS = 4
M, CI, CJ, NK = 4, 4, 16, 128
NI, NJ = 128, 256
GX, GY = 32, 16
PAIRS = ((0, 0), (0, 1), (0, 2), (1, 1), (1, 2), (2, 2))


def ring(size):
    return sorted(range(1, size), key=lambda a: -min(a, size - a))


def hops_gx(a):
    z, x = a // 4, a % 4
    return min(z, 8 - z) + min(x, 4 - x)


STAGE_GX = sorted(range(1, GX), key=lambda a: -hops_gx(a))
STAGE_GY = ring(GY)

GREETED = (
    [(0, dx, 0, 0) for dx in (1, 2, 3)]
    + [(dz, 0, 0, 0) for dz in (1, 2, 6, 7)]
    + [(0, 0, dy, 0) for dy in (1, 2, 6, 7)]
    + [(0, 0, 0, 1)]
)
TOLD = (
    [(dz, 0, 0, 0) for dz in (2, 6, 1, 7)] + [(0, 0, dy, 0) for dy in (2, 6, 1, 7)] + [(0, 0, 0, 1)],
    [(dz, 0, 0, 0) for dz in (4, 3, 5)] + [(0, 0, dy, 0) for dy in (4, 3, 5)],
)


def roll_lanes(value, shift):
    return pltpu.roll(value, shift % NK, value.ndim - 1)


def kernel(
    d_hbm, rate_hbm, out_ref, entry_ref,
    d_ref, rate_ref, dpad, upad, from_lo, from_hi, col_out, col_in, cor_out, cor_in, strip,
    rows, total, slots_gx, slots_gy,
    x_send, x_recv, y_send, y_recv, c_send, c_recv, r_send, r_recv, load, known,
):
    gx, gy = lax.axis_index("gx"), lax.axis_index("gy")
    z, x, y, core = lax.div(gx, 4), lax.rem(gx, 4), lax.div(gy, 2), lax.rem(gy, 2)
    first_i, first_j = gx * CI, gy * CJ
    has_x = (gx > 0, gx < GX - 1)
    has_y = (gy > 0, gy < GY - 1)
    step = (-1, 1)

    def at(dx, dy):
        return (gx + dx, gy + dy)

    def offset(dz, dx, dy, dc):
        return (
            lax.rem(z + dz, GX // 4) * 4 + lax.rem(x + dx, 4),
            lax.rem(y + dy, GY // 2) * 2 + lax.rem(core + dc, 2),
        )

    barrier = pltpu.get_barrier_semaphore()
    for sx in range(2):
        @pl.when(has_x[sx])
        def _(sx=sx):
            pl.semaphore_signal(barrier, inc=1, device_id=at(step[sx], 0), device_id_type=MESH)
    for sy in range(2):
        @pl.when(has_y[sy])
        def _(sy=sy):
            pl.semaphore_signal(barrier, inc=1, device_id=at(0, step[sy]), device_id_type=MESH)
    for sx, sy in itertools.product((0, 1), (0, 1)):
        @pl.when(has_x[sx] & has_y[sy])
        def _(sx=sx, sy=sy):
            pl.semaphore_signal(barrier, inc=1, device_id=at(step[sx], step[sy]), device_id_type=MESH)
    for o in GREETED:
        pl.semaphore_signal(barrier, inc=1, device_id=offset(*o), device_id_type=MESH)

    loads = [
        pltpu.make_async_copy(d_hbm, d_ref, load.at[0]),
        pltpu.make_async_copy(rate_hbm, rate_ref, load.at[1]),
    ]
    for copy in loads:
        copy.start()
    for copy in loads:
        copy.wait()

    for sy, (near, far) in enumerate(((0, 1), (CJ - 1, CJ - 2))):
        for m in range(M):
            for r in range(CI):
                col_out[sy, m, r : r + 1] = d_ref[m, r, near : near + 1]
                col_out[sy, m, CI + r : CI + r + 1] = d_ref[m, r, far : far + 1]
            for sx, r0 in enumerate((0, CI - 2)):
                for q in range(2):
                    cor_out[sx, sy, 2 * m + q : 2 * m + q + 1] = d_ref[m, r0 + q, near : near + 1]

    n_x = (gx > 0).astype(jnp.int32) + (gx < GX - 1).astype(jnp.int32)
    n_y = (gy > 0).astype(jnp.int32) + (gy < GY - 1).astype(jnp.int32)
    pl.semaphore_wait(barrier, len(GREETED) + n_x + n_y + n_x * n_y)

    def x_copy(sx, m):
        dst = (from_hi, from_lo)[sx]
        return pltpu.make_async_remote_copy(
            src_ref=d_ref.at[m], dst_ref=dst.at[m], send_sem=x_send.at[sx, m], recv_sem=x_recv.at[1 - sx, m],
            device_id=at(step[sx], 0), device_id_type=MESH,
        )

    def y_copy(sy):
        return pltpu.make_async_remote_copy(
            src_ref=col_out.at[sy], dst_ref=col_in.at[1 - sy], send_sem=y_send.at[sy], recv_sem=y_recv.at[1 - sy],
            device_id=at(0, step[sy]), device_id_type=MESH,
        )

    def c_copy(sx, sy):
        return pltpu.make_async_remote_copy(
            src_ref=cor_out.at[sx, sy], dst_ref=cor_in.at[1 - sx, 1 - sy],
            send_sem=c_send.at[sx, sy], recv_sem=c_recv.at[1 - sx, 1 - sy],
            device_id=at(step[sx], step[sy]), device_id_type=MESH,
        )

    def incoming_x(sx, m):
        dst = (from_lo, from_hi)[sx]
        return pltpu.make_async_remote_copy(
            src_ref=d_ref.at[m], dst_ref=dst.at[m], send_sem=x_send.at[sx, m], recv_sem=x_recv.at[sx, m],
            device_id=at(step[sx], 0), device_id_type=MESH,
        )

    def incoming_y(sy):
        return pltpu.make_async_remote_copy(
            src_ref=col_out.at[sy], dst_ref=col_in.at[sy], send_sem=y_send.at[sy], recv_sem=y_recv.at[sy],
            device_id=at(0, step[sy]), device_id_type=MESH,
        )

    def incoming_c(sx, sy):
        return pltpu.make_async_remote_copy(
            src_ref=cor_out.at[sx, sy], dst_ref=cor_in.at[sx, sy],
            send_sem=c_send.at[sx, sy], recv_sem=c_recv.at[sx, sy],
            device_id=at(step[sx], step[sy]), device_id_type=MESH,
        )

    for sy in range(2):
        @pl.when(has_y[sy])
        def _(sy=sy):
            y_copy(sy).start()
    for sx, sy in itertools.product((0, 1), (0, 1)):
        @pl.when(has_x[sx] & has_y[sy])
        def _(sx=sx, sy=sy):
            c_copy(sx, sy).start()
    for m in range(M):
        for sx in range(2):
            @pl.when(has_x[sx])
            def _(sx=sx, m=m):
                x_copy(sx, m).start()

    for o in TOLD[0]:
        pl.semaphore_signal(known.at[0], inc=1, device_id=offset(*o), device_id_type=MESH)

    lane = lax.broadcasted_iota(jnp.int32, (1, NK), 1)
    k_row = lane.astype(F32)
    not_first = (lane > 0).astype(F32)
    j_col = (first_j + lax.broadcasted_iota(jnp.int32, (CJ, NK), 0)).astype(F32)
    lam_row = jnp.ones((1, NK), F32)
    rates = []
    for m in range(M):
        c = [rate_ref[m, r] for r in range(9)]
        lam = c[0] + 127.0 * c[1] + c[2] + 255.0 * c[3] + 8001.0 * c[4] + 127.0 * (c[5] + c[6])
        lam_row = jnp.where(lane == m, lam, lam_row)
        rates.append(c)
    inv_row = 1.0 / lam_row

    def coefficients(m):
        inv = inv_row[0, m]
        c = [rates[m][r] * inv for r in range(7)] + rates[m][7:]
        ratio_j = j_col / c[7]
        ratio_k = k_row / c[8]
        make_u = c[0] / (1.0 + ratio_j * ratio_j)
        make_v = c[2] / (1.0 + ratio_k * ratio_k)
        gain_j = c[3] * (j_col + 1.0)
        loss = make_u + make_v + c[3] * j_col + (c[5] + c[6]) * k_row
        return c, make_u, make_v, gain_j, loss

    def row_scalars(c, r):
        i = (first_i + r).astype(F32)
        down = c[1] * (i + 1.0)
        pair = 0.5 * c[4] * (i + 2.0) * (i + 1.0)
        out = c[1] * i + 0.5 * c[4] * i * (i - 1.0)
        return down, pair, out

    def image(c, make_u, make_v, gain_j, loss, scalars, before2, before, here, after, after2, left, right):
        down, pair, out = scalars
        result = make_u * before + down * after + make_v * left + gain_j * right
        result = result + roll_lanes(after2, 1) * (pair * not_first)
        result = result + roll_lanes((c[5] * before2 + c[6] * here) * k_row, -1)
        return result - (loss + out) * here

    for sx in range(2):
        @pl.when(jnp.logical_not(has_x[sx]))
        def _(sx=sx):
            (from_lo, from_hi)[sx][...] = jnp.zeros_like(from_lo)
    for sy in range(2):
        @pl.when(jnp.logical_not(has_y[sy]))
        def _(sy=sy):
            col_in[sy] = jnp.zeros_like(col_in[sy])
    for sx, sy in itertools.product((0, 1), (0, 1)):
        @pl.when(jnp.logical_not(has_x[sx] & has_y[sy]))
        def _(sx=sx, sy=sy):
            cor_in[sx, sy] = jnp.zeros_like(cor_in[sx, sy])

    for m in range(M):
        for r in range(CI):
            dpad[m, r + 2, 8 : 8 + CJ] = d_ref[m, r]

    pl.semaphore_wait(known.at[0], len(TOLD[0]))
    for o in TOLD[1]:
        pl.semaphore_signal(known.at[1], inc=1, device_id=offset(*o), device_id_type=MESH)

    for sy in range(2):
        @pl.when(has_y[sy])
        def _(sy=sy):
            incoming_y(sy).wait_recv()
    for sx, sy in itertools.product((0, 1), (0, 1)):
        @pl.when(has_x[sx] & has_y[sy])
        def _(sx=sx, sy=sy):
            incoming_c(sx, sy).wait_recv()

    for m in range(M):
        for sy, at_col in enumerate((7, 8 + CJ)):
            for r in range(CI):
                dpad[m, r + 2, at_col : at_col + 1] = col_in[sy, m, r : r + 1]
            strip[m, sy, 2 : 2 + CI] = col_in[sy, m, 0:CI]
            for sx, r0 in enumerate((0, CI + 2)):
                strip[m, sy, r0 : r0 + 2] = cor_in[sx, sy, 2 * m : 2 * m + 2]
                for q in range(2):
                    dpad[m, r0 + q, at_col : at_col + 1] = cor_in[sx, sy, 2 * m + q : 2 * m + q + 1]

    inside_hi = (gx < GX - 1).astype(F32)
    for m in range(M):
        c, make_u, make_v, gain_j, loss = coefficients(m)
        for sx in range(2):
            @pl.when(has_x[sx])
            def _(sx=sx, m=m):
                incoming_x(sx, m).wait_recv()
        for q in range(2):
            dpad[m, q, 8 : 8 + CJ] = from_lo[m, 2 + q]
            dpad[m, CI + 2 + q, 8 : 8 + CJ] = from_hi[m, q]

        def full(r):
            if r < 0:
                return from_lo[m, CI + r]
            if r >= CI:
                return from_hi[m, r - CI]
            return d_ref[m, r]

        for r in range(-2, CI + 2):
            u = image(
                c, make_u, make_v, gain_j, loss, row_scalars(c, r),
                full(r - 2), full(r - 1), full(r), full(r + 1), full(r + 2),
                dpad[m, r + 2, 7 : 7 + CJ], dpad[m, r + 2, 9 : 9 + CJ],
            )
            if r >= CI:
                u = u * inside_hi
            upad[m, r + 2, 8 : 8 + CJ] = u

        i4 = (first_i + lax.broadcasted_iota(jnp.int32, (CI, NK), 0)).astype(F32)
        scalars = (
            c[1] * (i4 + 1.0),
            0.5 * c[4] * (i4 + 2.0) * (i4 + 1.0),
            c[1] * i4 + 0.5 * c[4] * i4 * (i4 - 1.0),
        )
        for sy, (jj, at_col) in enumerate(((-1, 7), (CJ, 8 + CJ))):
            j = jnp.full((1, NK), (first_j + jj).astype(F32))
            ratio = j / c[7]
            mu = c[0] / (1.0 + ratio * ratio)
            lo = mu + make_v + c[3] * j + (c[5] + c[6]) * k_row
            inner, outer = col_out[sy, m, 0:CI], col_in[sy, m, CI : 2 * CI]
            left, right = (outer, inner) if sy == 0 else (inner, outer)
            u = image(
                c, mu, make_v, c[3] * (j + 1.0), lo, scalars,
                strip[m, sy, 0:4], strip[m, sy, 1:5], strip[m, sy, 2:6], strip[m, sy, 3:7], strip[m, sy, 4:8],
                left, right,
            )
            if sy == 1:
                u = u * (gy < GY - 1).astype(F32)
            for r in range(CI):
                upad[m, r + 2, at_col : at_col + 1] = u[r : r + 1]

        sums = [jnp.zeros((8, NK), F32) for _ in PAIRS]
        for r in range(CI):
            mid = lambda q: upad[m, q + 2, 8 : 8 + CJ]
            u2 = image(
                c, make_u, make_v, gain_j, loss, row_scalars(c, r),
                mid(r - 2), mid(r - 1), mid(r), mid(r + 1), mid(r + 2),
                upad[m, r + 2, 7 : 7 + CJ], upad[m, r + 2, 9 : 9 + CJ],
            )
            out_ref[m, r] = u2
            basis = (d_ref[m, r], mid(r), u2)
            for p, (a, b) in enumerate(PAIRS):
                product = basis[a] * basis[b]
                sums[p] = sums[p] + product[0:8] + product[8:16]
        for p in range(len(PAIRS)):
            rows[p * M + m : p * M + m + 1] = jnp.sum(sums[p], axis=0, keepdims=True)

    n_rows = len(PAIRS) * M
    column = jnp.sum(rows[...], axis=1, keepdims=True)
    lanes = lax.broadcasted_iota(jnp.int32, (n_rows, NK), 1)
    places = lax.broadcasted_iota(jnp.int32, (n_rows, NK), 0)
    acc = jnp.sum(jnp.where(lanes == places, column, 0.0), axis=0, keepdims=True)

    pl.semaphore_wait(known.at[1], len(TOLD[1]))
    for stage, (offsets, slots) in enumerate(((STAGE_GX, slots_gx), (STAGE_GY, slots_gy))):
        total[stage] = acc
        for a in offsets:
            peer = (lax.rem(gx + a, GX), gy) if stage == 0 else (gx, lax.rem(gy + a, GY))
            pltpu.make_async_remote_copy(
                src_ref=total.at[stage], dst_ref=slots.at[a - 1], send_sem=r_send.at[stage], recv_sem=r_recv.at[stage],
                device_id=peer, device_id_type=MESH,
            ).start()
        whole = pltpu.make_async_remote_copy(
            src_ref=slots, dst_ref=slots, send_sem=r_send.at[stage], recv_sem=r_recv.at[stage],
            device_id=(lax.rem(gx + 1, GX), gy), device_id_type=MESH,
        )
        whole.wait_recv()
        acc = acc + jnp.sum(slots[...], axis=0)
        whole.wait_send()

    picked = [acc if p == 0 else roll_lanes(acc, -M * p) for p in range(len(PAIRS))]
    ok = lane < M
    picked = [jnp.where(ok, value, 1.0) for value in picked]
    scale = 1.0 / picked[0]
    a1, a2, b11, b12, b22 = [value * scale for value in picked[1:]]
    h00 = a1
    n1 = b11 - h00 * h00
    h10 = jnp.sqrt(n1)
    e = a2 - h00 * a1
    h01 = e / h10
    h11 = ((b12 - h00 * b11) - h00 * e) / n1
    ss = (b22 - h00 * b12) - h00 * (b12 - h00 * b11)
    h21 = jnp.sqrt(ss / n1 - h01 * h01 - h11 * h11)

    step_scale = lam_row * TAU
    entries = [step_scale * h for h in (h00, h10, h01, h11, h21)]
    small = 1.0 / 2.0**SQUARINGS
    g00, g10, g01, g11, g21 = [entry * small for entry in entries]
    one, zero = jnp.ones_like(h00), jnp.zeros_like(h00)
    p00, p01, p10, p11 = one, zero, zero, one
    w0 = w1 = zero
    for term in range(TAYLOR_TERMS, 0, -1):
        f = 1.0 / term
        w0, w1 = g21 * f * p10, g21 * f * p11
        q00 = 1.0 + (g00 * f * p00 + g01 * f * p10)
        q01 = g00 * f * p01 + g01 * f * p11
        q10 = g10 * f * p00 + g11 * f * p10
        q11 = 1.0 + (g10 * f * p01 + g11 * f * p11)
        p00, p01, p10, p11 = q00, q01, q10, q11
    for _ in range(SQUARINGS):
        w0, w1 = w0 + (w0 * p00 + w1 * p10), w1 + (w0 * p01 + w1 * p11)
        q00 = p00 * p00 + p01 * p10
        q01 = p00 * p01 + p01 * p11
        q10 = p10 * p00 + p11 * p10
        q11 = p10 * p01 + p11 * p11
        p00, p01, p10, p11 = q00, q01, q10, q11
    e0, e1, e2 = p00, p10, w0
    inv10 = 1.0 / h10
    e2 = e2 / h21
    f0 = e0 - e1 * h00 * inv10 + e2 * (h11 * h00 * inv10 - h01)
    f1 = (e1 - e2 * (h00 + h11)) * inv10
    f2 = e2 * inv10

    eye = lax.broadcasted_iota(jnp.int32, (8, NK), 0) == lax.broadcasted_iota(jnp.int32, (8, NK), 1)
    lanes8 = lax.broadcasted_iota(jnp.int32, (8, NK), 1)
    table = jnp.zeros((8, NK), F32)
    for q, entry in enumerate(entries):
        column = jnp.sum(jnp.where(eye, entry, 0.0), axis=1, keepdims=True)
        table = jnp.where(lanes8 == q, column, table)
    entry_ref[...] = table[:M, :5]

    for m in range(M):
        s0, s1, s2 = (jnp.broadcast_to(f[:, m : m + 1], (CJ, NK)) for f in (f0, f1, f2))
        for r in range(CI):
            out_ref[m, r] = s0 * d_ref[m, r] + s1 * upad[m, r + 2, 8 : 8 + CJ] + s2 * out_ref[m, r]

    for sy in range(2):
        @pl.when(has_y[sy])
        def _(sy=sy):
            y_copy(sy).wait_send()
    for sx, sy in itertools.product((0, 1), (0, 1)):
        @pl.when(has_x[sx] & has_y[sy])
        def _(sx=sx, sy=sy):
            c_copy(sx, sy).wait_send()
    for m in range(M):
        for sx in range(2):
            @pl.when(has_x[sx])
            def _(sx=sx, m=m):
                x_copy(sx, m).wait_send()


def shards(density, rate_table):
    vmem = functools.partial(pltpu.VMEM, dtype=F32)
    dma = pltpu.SemaphoreType.DMA
    return pl.pallas_call(
        kernel,
        out_shape=(pltpu.VMEM(density.shape, F32), pltpu.VMEM((M, 5), F32)),
        in_specs=[pl.BlockSpec(memory_space=pl.ANY), pl.BlockSpec(memory_space=pl.ANY)],
        out_specs=(pl.BlockSpec(memory_space=pltpu.VMEM), pl.BlockSpec(memory_space=pltpu.VMEM)),
        scratch_shapes=[
            vmem((M, CI, CJ, NK)),
            pltpu.SMEM((M, 9), F32),
            vmem((M, CI + 4, 32, NK)),
            vmem((M, CI + 4, 32, NK)),
            vmem((M, CI, CJ, NK)),
            vmem((M, CI, CJ, NK)),
            vmem((2, M, 8, NK)),
            vmem((2, M, 8, NK)),
            vmem((2, 2, 8, NK)),
            vmem((2, 2, 8, NK)),
            vmem((M, 2, 8, NK)),
            vmem((len(PAIRS) * M, NK)),
            vmem((2, 1, NK)),
            vmem((GX - 1, 1, NK)),
            vmem((GY - 1, 1, NK)),
            dma((2, M)),
            dma((2, M)),
            dma((2,)),
            dma((2,)),
            dma((2, 2)),
            dma((2, 2)),
            dma((2,)),
            dma((2,)),
            dma((2,)),
            pltpu.SemaphoreType.REGULAR((2,)),
        ],
        compiler_params=pltpu.CompilerParams(collective_id=0, has_side_effects=True),
    )(density, rate_table)


def solution(mesh):
    specs = (P(None, "gx", "gy", None), P())
    return jax.shard_map(shards, mesh=mesh, in_specs=specs, out_specs=specs, check_vma=False)
```

```python
import functools
import itertools

import jax
import jax.numpy as jnp
from jax import lax
from jax.experimental import pallas as pl
from jax.experimental.pallas import tpu as pltpu
from jax.sharding import PartitionSpec as P

MESH = pl.DeviceIdType.MESH
F32 = jnp.float32
TAU = 0.01
TAYLOR_TERMS = 16
SQUARINGS = 4
M, CI, CJ, NK = 4, 4, 16, 128
NI, NJ = 128, 256
GX, GY = 32, 16
PAIRS = ((0, 0), (0, 1), (0, 2), (1, 1), (1, 2), (2, 2))


def ring(size):
    return sorted(range(1, size), key=lambda a: -min(a, size - a))


def hops_gx(a):
    z, x = a // 4, a % 4
    return min(z, 8 - z) + min(x, 4 - x)


STAGE_GX = sorted(range(1, GX), key=lambda a: -hops_gx(a))
STAGE_GY = ring(GY)

GREETED = (
    [(0, dx, 0, 0) for dx in (1, 3)]
    + [(0, 0, dy, c) for dy in (1, 7) for c in (1, 0)]
    + [(dz, 0, 0, 0) for dz in (1, 7)]
    + [(0, 0, 0, 1)]
)
TOLD = (
    GREETED,
    [(dz, 0, 0, 0) for dz in (2, 6, 1, 7)] + [(0, 0, dy, 0) for dy in (2, 6)],
    [(dz, 0, 0, 0) for dz in (2, 6)],
)


def roll_lanes(value, shift):
    return pltpu.roll(value, shift % NK, value.ndim - 1)


def kernel(
    d_hbm, rate_hbm, out_ref, entry_ref,
    d_ref, rate_ref, dpad, upad, from_lo, from_hi, col_out, col_in, cor_out, cor_in, strip,
    rows, total, slots_gx, slots_gy,
    x_send, x_recv, y_send, y_recv, c_send, c_recv, r_send, r_recv, load, known,
):
    gx, gy = lax.axis_index("gx"), lax.axis_index("gy")
    z, x, y, core = lax.div(gx, 4), lax.rem(gx, 4), lax.div(gy, 2), lax.rem(gy, 2)
    first_i, first_j = gx * CI, gy * CJ
    has_x = (gx > 0, gx < GX - 1)
    has_y = (gy > 0, gy < GY - 1)
    step = (-1, 1)
    has_edge = ((x == 0) & has_x[0], (x == 3) & has_x[1])

    def at(dx, dy):
        return (gx + dx, gy + dy)

    def offset(dz, dx, dy, dc):
        return (
            lax.rem(z + dz, GX // 4) * 4 + lax.rem(x + dx, 4),
            lax.rem(y + dy, GY // 2) * 2 + lax.rem(core + dc, 2),
        )

    barrier = pltpu.get_barrier_semaphore()
    for sx in range(2):
        @pl.when(has_edge[sx])
        def _(sx=sx):
            pl.semaphore_signal(barrier, inc=1, device_id=at(step[sx], 0), device_id_type=MESH)
    for o in GREETED:
        pl.semaphore_signal(barrier, inc=1, device_id=offset(*o), device_id_type=MESH)

    loads = [
        pltpu.make_async_copy(d_hbm, d_ref, load.at[0]),
        pltpu.make_async_copy(rate_hbm, rate_ref, load.at[1]),
    ]
    for copy in loads:
        copy.start()
    for copy in loads:
        copy.wait()

    for sy, (near, far) in enumerate(((0, 1), (CJ - 1, CJ - 2))):
        for m in range(M):
            for r in range(CI):
                col_out[sy, m, r : r + 1] = d_ref[m, r, near : near + 1]
                col_out[sy, m, CI + r : CI + r + 1] = d_ref[m, r, far : far + 1]
            for sx, r0 in enumerate((0, CI - 2)):
                for q in range(2):
                    cor_out[sx, sy, 2 * m + q : 2 * m + q + 1] = d_ref[m, r0 + q, near : near + 1]

    n_edge = has_edge[0].astype(jnp.int32) + has_edge[1].astype(jnp.int32)
    pl.semaphore_wait(barrier, len(GREETED) + n_edge)

    def x_copy(sx, m):
        dst = (from_hi, from_lo)[sx]
        return pltpu.make_async_remote_copy(
            src_ref=d_ref.at[m], dst_ref=dst.at[m], send_sem=x_send.at[sx, m], recv_sem=x_recv.at[1 - sx, m],
            device_id=at(step[sx], 0), device_id_type=MESH,
        )

    def y_copy(sy):
        return pltpu.make_async_remote_copy(
            src_ref=col_out.at[sy], dst_ref=col_in.at[1 - sy], send_sem=y_send.at[sy], recv_sem=y_recv.at[1 - sy],
            device_id=at(0, step[sy]), device_id_type=MESH,
        )

    def c_copy(sx, sy):
        return pltpu.make_async_remote_copy(
            src_ref=cor_out.at[sx, sy], dst_ref=cor_in.at[1 - sx, 1 - sy],
            send_sem=c_send.at[sx, sy], recv_sem=c_recv.at[1 - sx, 1 - sy],
            device_id=at(step[sx], step[sy]), device_id_type=MESH,
        )

    def incoming_x(sx, m):
        dst = (from_lo, from_hi)[sx]
        return pltpu.make_async_remote_copy(
            src_ref=d_ref.at[m], dst_ref=dst.at[m], send_sem=x_send.at[sx, m], recv_sem=x_recv.at[sx, m],
            device_id=at(step[sx], 0), device_id_type=MESH,
        )

    def incoming_y(sy):
        return pltpu.make_async_remote_copy(
            src_ref=col_out.at[sy], dst_ref=col_in.at[sy], send_sem=y_send.at[sy], recv_sem=y_recv.at[sy],
            device_id=at(0, step[sy]), device_id_type=MESH,
        )

    def incoming_c(sx, sy):
        return pltpu.make_async_remote_copy(
            src_ref=cor_out.at[sx, sy], dst_ref=cor_in.at[sx, sy],
            send_sem=c_send.at[sx, sy], recv_sem=c_recv.at[sx, sy],
            device_id=at(step[sx], step[sy]), device_id_type=MESH,
        )

    for sy in range(2):
        @pl.when(has_y[sy])
        def _(sy=sy):
            y_copy(sy).start()
    for m in range(M):
        for sx in range(2):
            @pl.when(has_x[sx])
            def _(sx=sx, m=m):
                x_copy(sx, m).start()

    def tell(level):
        for o in TOLD[level]:
            pl.semaphore_signal(known.at[level], inc=1, device_id=offset(*o), device_id_type=MESH)

    tell(0)

    lane = lax.broadcasted_iota(jnp.int32, (1, NK), 1)
    k_row = lane.astype(F32)
    not_first = (lane > 0).astype(F32)
    j_col = (first_j + lax.broadcasted_iota(jnp.int32, (CJ, NK), 0)).astype(F32)
    lam_row = jnp.ones((1, NK), F32)
    rates = []
    for m in range(M):
        c = [rate_ref[m, r] for r in range(9)]
        lam = c[0] + 127.0 * c[1] + c[2] + 255.0 * c[3] + 8001.0 * c[4] + 127.0 * (c[5] + c[6])
        lam_row = jnp.where(lane == m, lam, lam_row)
        rates.append(c)
    inv_row = 1.0 / lam_row

    def coefficients(m):
        inv = inv_row[0, m]
        c = [rates[m][r] * inv for r in range(7)] + rates[m][7:]
        ratio_j = j_col / c[7]
        ratio_k = k_row / c[8]
        make_u = c[0] / (1.0 + ratio_j * ratio_j)
        make_v = c[2] / (1.0 + ratio_k * ratio_k)
        gain_j = c[3] * (j_col + 1.0)
        loss = make_u + make_v + c[3] * j_col + (c[5] + c[6]) * k_row
        return c, make_u, make_v, gain_j, loss

    def row_scalars(c, r):
        i = (first_i + r).astype(F32)
        down = c[1] * (i + 1.0)
        pair = 0.5 * c[4] * (i + 2.0) * (i + 1.0)
        out = c[1] * i + 0.5 * c[4] * i * (i - 1.0)
        return down, pair, out

    def image(c, make_u, make_v, gain_j, loss, scalars, before2, before, here, after, after2, left, right):
        down, pair, out = scalars
        result = make_u * before + down * after + make_v * left + gain_j * right
        result = result + roll_lanes(after2, 1) * (pair * not_first)
        result = result + roll_lanes((c[5] * before2 + c[6] * here) * k_row, -1)
        return result - (loss + out) * here

    for sx in range(2):
        @pl.when(jnp.logical_not(has_x[sx]))
        def _(sx=sx):
            (from_lo, from_hi)[sx][...] = jnp.zeros_like(from_lo)
    for sy in range(2):
        @pl.when(jnp.logical_not(has_y[sy]))
        def _(sy=sy):
            col_in[sy] = jnp.zeros_like(col_in[sy])
    for sx, sy in itertools.product((0, 1), (0, 1)):
        @pl.when(jnp.logical_not(has_x[sx] & has_y[sy]))
        def _(sx=sx, sy=sy):
            cor_in[sx, sy] = jnp.zeros_like(cor_in[sx, sy])

    for m in range(M):
        for r in range(CI):
            dpad[m, r + 2, 8 : 8 + CJ] = d_ref[m, r]

    pl.semaphore_wait(known.at[0], len(TOLD[0]))
    for sx, sy in itertools.product((0, 1), (0, 1)):
        @pl.when(has_x[sx] & has_y[sy])
        def _(sx=sx, sy=sy):
            c_copy(sx, sy).start()
    tell(1)
    pl.semaphore_wait(known.at[1], len(TOLD[1]))
    tell(2)

    for sy in range(2):
        @pl.when(has_y[sy])
        def _(sy=sy):
            incoming_y(sy).wait_recv()
    for sx, sy in itertools.product((0, 1), (0, 1)):
        @pl.when(has_x[sx] & has_y[sy])
        def _(sx=sx, sy=sy):
            incoming_c(sx, sy).wait_recv()

    for m in range(M):
        for sy, at_col in enumerate((7, 8 + CJ)):
            for r in range(CI):
                dpad[m, r + 2, at_col : at_col + 1] = col_in[sy, m, r : r + 1]
            strip[m, sy, 2 : 2 + CI] = col_in[sy, m, 0:CI]
            for sx, r0 in enumerate((0, CI + 2)):
                strip[m, sy, r0 : r0 + 2] = cor_in[sx, sy, 2 * m : 2 * m + 2]
                for q in range(2):
                    dpad[m, r0 + q, at_col : at_col + 1] = cor_in[sx, sy, 2 * m + q : 2 * m + q + 1]

    inside_hi = (gx < GX - 1).astype(F32)
    for m in range(M):
        c, make_u, make_v, gain_j, loss = coefficients(m)
        for sx in range(2):
            @pl.when(has_x[sx])
            def _(sx=sx, m=m):
                incoming_x(sx, m).wait_recv()
        for q in range(2):
            dpad[m, q, 8 : 8 + CJ] = from_lo[m, 2 + q]
            dpad[m, CI + 2 + q, 8 : 8 + CJ] = from_hi[m, q]

        def full(r):
            if r < 0:
                return from_lo[m, CI + r]
            if r >= CI:
                return from_hi[m, r - CI]
            return d_ref[m, r]

        for r in range(-2, CI + 2):
            u = image(
                c, make_u, make_v, gain_j, loss, row_scalars(c, r),
                full(r - 2), full(r - 1), full(r), full(r + 1), full(r + 2),
                dpad[m, r + 2, 7 : 7 + CJ], dpad[m, r + 2, 9 : 9 + CJ],
            )
            if r >= CI:
                u = u * inside_hi
            upad[m, r + 2, 8 : 8 + CJ] = u

        i4 = (first_i + lax.broadcasted_iota(jnp.int32, (CI, NK), 0)).astype(F32)
        scalars = (
            c[1] * (i4 + 1.0),
            0.5 * c[4] * (i4 + 2.0) * (i4 + 1.0),
            c[1] * i4 + 0.5 * c[4] * i4 * (i4 - 1.0),
        )
        for sy, (jj, at_col) in enumerate(((-1, 7), (CJ, 8 + CJ))):
            j = jnp.full((1, NK), (first_j + jj).astype(F32))
            ratio = j / c[7]
            mu = c[0] / (1.0 + ratio * ratio)
            lo = mu + make_v + c[3] * j + (c[5] + c[6]) * k_row
            inner, outer = col_out[sy, m, 0:CI], col_in[sy, m, CI : 2 * CI]
            left, right = (outer, inner) if sy == 0 else (inner, outer)
            u = image(
                c, mu, make_v, c[3] * (j + 1.0), lo, scalars,
                strip[m, sy, 0:4], strip[m, sy, 1:5], strip[m, sy, 2:6], strip[m, sy, 3:7], strip[m, sy, 4:8],
                left, right,
            )
            if sy == 1:
                u = u * (gy < GY - 1).astype(F32)
            for r in range(CI):
                upad[m, r + 2, at_col : at_col + 1] = u[r : r + 1]

        sums = [jnp.zeros((8, NK), F32) for _ in PAIRS]
        for r in range(CI):
            mid = lambda q: upad[m, q + 2, 8 : 8 + CJ]
            u2 = image(
                c, make_u, make_v, gain_j, loss, row_scalars(c, r),
                mid(r - 2), mid(r - 1), mid(r), mid(r + 1), mid(r + 2),
                upad[m, r + 2, 7 : 7 + CJ], upad[m, r + 2, 9 : 9 + CJ],
            )
            out_ref[m, r] = u2
            basis = (d_ref[m, r], mid(r), u2)
            for p, (a, b) in enumerate(PAIRS):
                product = basis[a] * basis[b]
                sums[p] = sums[p] + product[0:8] + product[8:16]
        for p in range(len(PAIRS)):
            rows[p * M + m : p * M + m + 1] = jnp.sum(sums[p], axis=0, keepdims=True)

    n_rows = len(PAIRS) * M
    column = jnp.sum(rows[...], axis=1, keepdims=True)
    lanes = lax.broadcasted_iota(jnp.int32, (n_rows, NK), 1)
    places = lax.broadcasted_iota(jnp.int32, (n_rows, NK), 0)
    acc = jnp.sum(jnp.where(lanes == places, column, 0.0), axis=0, keepdims=True)

    sent = []
    for stage, (offsets, slots) in enumerate(((STAGE_GY, slots_gy), (STAGE_GX, slots_gx))):
        if stage == 1:
            pl.semaphore_wait(known.at[2], len(TOLD[2]))
        total[stage] = acc
        for a in offsets:
            peer = (gx, lax.rem(gy + a, GY)) if stage == 0 else (lax.rem(gx + a, GX), gy)
            pltpu.make_async_remote_copy(
                src_ref=total.at[stage], dst_ref=slots.at[a - 1], send_sem=r_send.at[stage], recv_sem=r_recv.at[stage],
                device_id=peer, device_id_type=MESH,
            ).start()
        whole = pltpu.make_async_remote_copy(
            src_ref=slots, dst_ref=slots, send_sem=r_send.at[stage], recv_sem=r_recv.at[stage],
            device_id=peer, device_id_type=MESH,
        )
        whole.wait_recv()
        acc = acc + jnp.sum(slots[...], axis=0)
        sent.append(whole)

    picked = [acc if p == 0 else roll_lanes(acc, -M * p) for p in range(len(PAIRS))]
    ok = lane < M
    picked = [jnp.where(ok, value, 1.0) for value in picked]
    scale = 1.0 / picked[0]
    a1, a2, b11, b12, b22 = [value * scale for value in picked[1:]]
    h00 = a1
    n1 = b11 - h00 * h00
    h10 = jnp.sqrt(n1)
    e = a2 - h00 * a1
    h01 = e / h10
    h11 = ((b12 - h00 * b11) - h00 * e) / n1
    ss = (b22 - h00 * b12) - h00 * (b12 - h00 * b11)
    h21 = jnp.sqrt(ss / n1 - h01 * h01 - h11 * h11)

    step_scale = lam_row * TAU
    entries = [step_scale * h for h in (h00, h10, h01, h11, h21)]
    small = 1.0 / 2.0**SQUARINGS
    g00, g10, g01, g11, g21 = [entry * small for entry in entries]
    one, zero = jnp.ones_like(h00), jnp.zeros_like(h00)
    p00, p01, p10, p11 = one, zero, zero, one
    w0 = w1 = zero
    for term in range(TAYLOR_TERMS, 0, -1):
        f = 1.0 / term
        w0, w1 = g21 * f * p10, g21 * f * p11
        q00 = 1.0 + (g00 * f * p00 + g01 * f * p10)
        q01 = g00 * f * p01 + g01 * f * p11
        q10 = g10 * f * p00 + g11 * f * p10
        q11 = 1.0 + (g10 * f * p01 + g11 * f * p11)
        p00, p01, p10, p11 = q00, q01, q10, q11
    for _ in range(SQUARINGS):
        w0, w1 = w0 + (w0 * p00 + w1 * p10), w1 + (w0 * p01 + w1 * p11)
        q00 = p00 * p00 + p01 * p10
        q01 = p00 * p01 + p01 * p11
        q10 = p10 * p00 + p11 * p10
        q11 = p10 * p01 + p11 * p11
        p00, p01, p10, p11 = q00, q01, q10, q11
    e0, e1, e2 = p00, p10, w0
    inv10 = 1.0 / h10
    e2 = e2 / h21
    f0 = e0 - e1 * h00 * inv10 + e2 * (h11 * h00 * inv10 - h01)
    f1 = (e1 - e2 * (h00 + h11)) * inv10
    f2 = e2 * inv10

    eye = lax.broadcasted_iota(jnp.int32, (8, NK), 0) == lax.broadcasted_iota(jnp.int32, (8, NK), 1)
    lanes8 = lax.broadcasted_iota(jnp.int32, (8, NK), 1)
    table = jnp.zeros((8, NK), F32)
    for q, entry in enumerate(entries):
        column = jnp.sum(jnp.where(eye, entry, 0.0), axis=1, keepdims=True)
        table = jnp.where(lanes8 == q, column, table)
    entry_ref[...] = table[:M, :5]

    for m in range(M):
        s0, s1, s2 = (jnp.broadcast_to(f[:, m : m + 1], (CJ, NK)) for f in (f0, f1, f2))
        for r in range(CI):
            out_ref[m, r] = s0 * d_ref[m, r] + s1 * upad[m, r + 2, 8 : 8 + CJ] + s2 * out_ref[m, r]

    for whole in sent:
        whole.wait_send()
    for sy in range(2):
        @pl.when(has_y[sy])
        def _(sy=sy):
            y_copy(sy).wait_send()
    for sx, sy in itertools.product((0, 1), (0, 1)):
        @pl.when(has_x[sx] & has_y[sy])
        def _(sx=sx, sy=sy):
            c_copy(sx, sy).wait_send()
    for m in range(M):
        for sx in range(2):
            @pl.when(has_x[sx])
            def _(sx=sx, m=m):
                x_copy(sx, m).wait_send()


def store(field_ref, entry_ref, field_out, entry_out, sems):
    copies = [
        pltpu.make_async_copy(field_ref, field_out, sems.at[0]),
        pltpu.make_async_copy(entry_ref, entry_out, sems.at[1]),
    ]
    for copy in copies:
        copy.start()
    for copy in copies:
        copy.wait()


def shards(density, rate_table):
    vmem = functools.partial(pltpu.VMEM, dtype=F32)
    dma = pltpu.SemaphoreType.DMA
    results = pl.pallas_call(
        kernel,
        out_shape=(pltpu.VMEM(density.shape, F32), pltpu.VMEM((M, 5), F32)),
        in_specs=[pl.BlockSpec(memory_space=pl.ANY), pl.BlockSpec(memory_space=pl.ANY)],
        out_specs=(pl.BlockSpec(memory_space=pltpu.VMEM), pl.BlockSpec(memory_space=pltpu.VMEM)),
        scratch_shapes=[
            vmem((M, CI, CJ, NK)),
            pltpu.SMEM((M, 9), F32),
            vmem((M, CI + 4, 32, NK)),
            vmem((M, CI + 4, 32, NK)),
            vmem((M, CI, CJ, NK)),
            vmem((M, CI, CJ, NK)),
            vmem((2, M, 8, NK)),
            vmem((2, M, 8, NK)),
            vmem((2, 2, 8, NK)),
            vmem((2, 2, 8, NK)),
            vmem((M, 2, 8, NK)),
            vmem((len(PAIRS) * M, NK)),
            vmem((2, 1, NK)),
            vmem((GX - 1, 1, NK)),
            vmem((GY - 1, 1, NK)),
            dma((2, M)),
            dma((2, M)),
            dma((2,)),
            dma((2,)),
            dma((2, 2)),
            dma((2, 2)),
            dma((2,)),
            dma((2,)),
            dma((2,)),
            pltpu.SemaphoreType.REGULAR((3,)),
        ],
        compiler_params=pltpu.CompilerParams(collective_id=0, has_side_effects=True),
    )(density, rate_table)
    return pl.pallas_call(
        store,
        out_shape=(jax.ShapeDtypeStruct(density.shape, F32), jax.ShapeDtypeStruct((M, 5), F32)),
        in_specs=[pl.BlockSpec(memory_space=pltpu.VMEM)] * 2,
        out_specs=(pl.BlockSpec(memory_space=pl.ANY),) * 2,
        scratch_shapes=[dma((2,))],
        compiler_params=pltpu.CompilerParams(vmem_limit_bytes=1 << 20),
    )(*results)


def solution(mesh):
    specs = (P(None, "gx", "gy", None), P())
    return jax.shard_map(shards, mesh=mesh, in_specs=specs, out_specs=specs, check_vma=False)
```

```python
import functools
import itertools

import jax
import jax.numpy as jnp
from jax import lax
from jax.experimental import pallas as pl
from jax.experimental.pallas import tpu as pltpu
from jax.sharding import PartitionSpec as P

MESH = pl.DeviceIdType.MESH
F32 = jnp.float32
TAU = 0.01
TAYLOR_TERMS = 16
SQUARINGS = 4
M, CI, CJ, NK = 4, 4, 16, 128
NI, NJ = 128, 256
GX, GY = 32, 16
PAIRS = ((0, 0), (0, 1), (0, 2), (1, 1), (1, 2), (2, 2))


def ring(size):
    return sorted(range(1, size), key=lambda a: -min(a, size - a))


def hops_gx(a):
    z, x = a // 4, a % 4
    return min(z, 8 - z) + min(x, 4 - x)


STAGE_GX = sorted(range(1, GX), key=lambda a: -hops_gx(a))
STAGE_GY = ring(GY)

GREETED = (
    [(0, dx, 0, 0) for dx in (1, 3)]
    + [(0, 0, dy, c) for dy in (1, 7) for c in (1, 0)]
    + [(dz, 0, 0, 0) for dz in (1, 7)]
    + [(0, 0, 0, 1)]
)
TOLD = (
    GREETED,
    [(dz, 0, 0, 0) for dz in (2, 6, 1, 7)] + [(0, 0, dy, 0) for dy in (2, 6)],
    [(dz, 0, 0, 0) for dz in (2, 6)],
)


FAR_Z = 4
N_FAR = (GX - 4 * FAR_Z) * GY
EARLY_REACH = 6


def is_early(gx, gy):
    z, x, y = gx // 4, gx % 4, gy // 2
    return (5 * y + 2 * x + 4 * z <= EARLY_REACH) & (gx + gy > 0)


EARLY = sorted(
    (p for p in itertools.product(range(GX), range(GY)) if is_early(*p)),
    key=lambda p: 5 * (p[1] // 2) + 2 * (p[0] % 4) + 4 * (p[0] // 4),
)
FAR = sorted(
    itertools.product(range(4 * FAR_Z, GX), range(GY)),
    key=lambda p: (abs(p[1] // 2 - 4), abs(p[0] % 4 - 2), p),
)


def roll_lanes(value, shift):
    return pltpu.roll(value, shift % NK, value.ndim - 1)


def kernel(
    d_hbm, rate_hbm, out_ref, entry_ref,
    d_ref, rate_ref, dpad, upad, from_lo, from_hi, col_out, col_in, cor_out, cor_in, strip,
    rows, total, slots_gx, slots_gy, direct,
    x_send, x_recv, y_send, y_recv, c_send, c_recv, r_send, r_recv, e_send, e_recv, load, known,
):
    gx, gy = lax.axis_index("gx"), lax.axis_index("gy")
    z, x, y, core = lax.div(gx, 4), lax.rem(gx, 4), lax.div(gy, 2), lax.rem(gy, 2)
    first_i, first_j = gx * CI, gy * CJ
    has_x = (gx > 0, gx < GX - 1)
    has_y = (gy > 0, gy < GY - 1)
    step = (-1, 1)
    has_edge = ((x == 0) & has_x[0], (x == 3) & has_x[1])

    def at(dx, dy):
        return (gx + dx, gy + dy)

    def offset(dz, dx, dy, dc):
        return (
            lax.rem(z + dz, GX // 4) * 4 + lax.rem(x + dx, 4),
            lax.rem(y + dy, GY // 2) * 2 + lax.rem(core + dc, 2),
        )

    barrier = pltpu.get_barrier_semaphore()
    for sx in range(2):
        @pl.when(has_edge[sx])
        def _(sx=sx):
            pl.semaphore_signal(barrier, inc=1, device_id=at(step[sx], 0), device_id_type=MESH)
    for sx, sy in itertools.product((0, 1), (0, 1)):
        @pl.when(has_x[sx] & has_y[sy])
        def _(sx=sx, sy=sy):
            pl.semaphore_signal(barrier, inc=1, device_id=at(step[sx], step[sy]), device_id_type=MESH)
    for o in GREETED:
        pl.semaphore_signal(barrier, inc=1, device_id=offset(*o), device_id_type=MESH)

    far, early = z >= FAR_Z, is_early(gx, gy)

    @pl.when(early)
    def _():
        for p in FAR:
            pl.semaphore_signal(barrier, inc=1, device_id=p, device_id_type=MESH)

    loads = [
        pltpu.make_async_copy(d_hbm, d_ref, load.at[0]),
        pltpu.make_async_copy(rate_hbm, rate_ref, load.at[1]),
    ]
    for copy in loads:
        copy.start()
    for copy in loads:
        copy.wait()

    for sy, (near, next_near) in enumerate(((0, 1), (CJ - 1, CJ - 2))):
        for m in range(M):
            for r in range(CI):
                col_out[sy, m, r : r + 1] = d_ref[m, r, near : near + 1]
                col_out[sy, m, CI + r : CI + r + 1] = d_ref[m, r, next_near : next_near + 1]
            for sx, r0 in enumerate((0, CI - 2)):
                for q in range(2):
                    cor_out[sx, sy, 2 * m + q : 2 * m + q + 1] = d_ref[m, r0 + q, near : near + 1]

    n_edge = has_edge[0].astype(jnp.int32) + has_edge[1].astype(jnp.int32)
    n_x = has_x[0].astype(jnp.int32) + has_x[1].astype(jnp.int32)
    n_y = has_y[0].astype(jnp.int32) + has_y[1].astype(jnp.int32)
    pl.semaphore_wait(barrier, len(GREETED) + n_edge + n_x * n_y + far.astype(jnp.int32) * len(EARLY))

    def x_copy(sx, m):
        dst = (from_hi, from_lo)[sx]
        return pltpu.make_async_remote_copy(
            src_ref=d_ref.at[m], dst_ref=dst.at[m], send_sem=x_send.at[sx, m], recv_sem=x_recv.at[1 - sx, m],
            device_id=at(step[sx], 0), device_id_type=MESH,
        )

    def y_copy(sy):
        return pltpu.make_async_remote_copy(
            src_ref=col_out.at[sy], dst_ref=col_in.at[1 - sy], send_sem=y_send.at[sy], recv_sem=y_recv.at[1 - sy],
            device_id=at(0, step[sy]), device_id_type=MESH,
        )

    def c_copy(sx, sy):
        return pltpu.make_async_remote_copy(
            src_ref=cor_out.at[sx, sy], dst_ref=cor_in.at[1 - sx, 1 - sy],
            send_sem=c_send.at[sx, sy], recv_sem=c_recv.at[1 - sx, 1 - sy],
            device_id=at(step[sx], step[sy]), device_id_type=MESH,
        )

    def incoming_x(sx, m):
        dst = (from_lo, from_hi)[sx]
        return pltpu.make_async_remote_copy(
            src_ref=d_ref.at[m], dst_ref=dst.at[m], send_sem=x_send.at[sx, m], recv_sem=x_recv.at[sx, m],
            device_id=at(step[sx], 0), device_id_type=MESH,
        )

    def incoming_y(sy):
        return pltpu.make_async_remote_copy(
            src_ref=col_out.at[sy], dst_ref=col_in.at[sy], send_sem=y_send.at[sy], recv_sem=y_recv.at[sy],
            device_id=at(0, step[sy]), device_id_type=MESH,
        )

    def incoming_c(sx, sy):
        return pltpu.make_async_remote_copy(
            src_ref=cor_out.at[sx, sy], dst_ref=cor_in.at[sx, sy],
            send_sem=c_send.at[sx, sy], recv_sem=c_recv.at[sx, sy],
            device_id=at(step[sx], step[sy]), device_id_type=MESH,
        )

    for sy in range(2):
        @pl.when(has_y[sy])
        def _(sy=sy):
            y_copy(sy).start()
    for sx, sy in itertools.product((0, 1), (0, 1)):
        @pl.when(has_x[sx] & has_y[sy])
        def _(sx=sx, sy=sy):
            c_copy(sx, sy).start()
    for m in range(M):
        for sx in range(2):
            @pl.when(has_x[sx])
            def _(sx=sx, m=m):
                x_copy(sx, m).start()

    def tell(level):
        for o in TOLD[level]:
            pl.semaphore_signal(known.at[level], inc=1, device_id=offset(*o), device_id_type=MESH)

    tell(0)

    lane = lax.broadcasted_iota(jnp.int32, (1, NK), 1)
    k_row = lane.astype(F32)
    not_first = (lane > 0).astype(F32)
    j_col = (first_j + lax.broadcasted_iota(jnp.int32, (CJ, NK), 0)).astype(F32)
    lam_row = jnp.ones((1, NK), F32)
    rates = []
    for m in range(M):
        c = [rate_ref[m, r] for r in range(9)]
        lam = c[0] + 127.0 * c[1] + c[2] + 255.0 * c[3] + 8001.0 * c[4] + 127.0 * (c[5] + c[6])
        lam_row = jnp.where(lane == m, lam, lam_row)
        rates.append(c)
    inv_row = 1.0 / lam_row

    def coefficients(m):
        inv = inv_row[0, m]
        c = [rates[m][r] * inv for r in range(7)] + rates[m][7:]
        ratio_j = j_col / c[7]
        ratio_k = k_row / c[8]
        make_u = c[0] / (1.0 + ratio_j * ratio_j)
        make_v = c[2] / (1.0 + ratio_k * ratio_k)
        gain_j = c[3] * (j_col + 1.0)
        loss = make_u + make_v + c[3] * j_col + (c[5] + c[6]) * k_row
        return c, make_u, make_v, gain_j, loss

    def row_scalars(c, r):
        i = (first_i + r).astype(F32)
        down = c[1] * (i + 1.0)
        pair = 0.5 * c[4] * (i + 2.0) * (i + 1.0)
        out = c[1] * i + 0.5 * c[4] * i * (i - 1.0)
        return down, pair, out

    def image(c, make_u, make_v, gain_j, loss, scalars, before2, before, here, after, after2, left, right):
        down, pair, out = scalars
        result = make_u * before + down * after + make_v * left + gain_j * right
        result = result + roll_lanes(after2, 1) * (pair * not_first)
        result = result + roll_lanes((c[5] * before2 + c[6] * here) * k_row, -1)
        return result - (loss + out) * here

    for sx in range(2):
        @pl.when(jnp.logical_not(has_x[sx]))
        def _(sx=sx):
            (from_lo, from_hi)[sx][...] = jnp.zeros_like(from_lo)
    for sy in range(2):
        @pl.when(jnp.logical_not(has_y[sy]))
        def _(sy=sy):
            col_in[sy] = jnp.zeros_like(col_in[sy])
    for sx, sy in itertools.product((0, 1), (0, 1)):
        @pl.when(jnp.logical_not(has_x[sx] & has_y[sy]))
        def _(sx=sx, sy=sy):
            cor_in[sx, sy] = jnp.zeros_like(cor_in[sx, sy])

    for m in range(M):
        for r in range(CI):
            dpad[m, r + 2, 8 : 8 + CJ] = d_ref[m, r]

    pl.semaphore_wait(known.at[0], len(TOLD[0]))
    tell(1)
    pl.semaphore_wait(known.at[1], len(TOLD[1]))
    tell(2)

    for sy in range(2):
        @pl.when(has_y[sy])
        def _(sy=sy):
            incoming_y(sy).wait_recv()
    for sx, sy in itertools.product((0, 1), (0, 1)):
        @pl.when(has_x[sx] & has_y[sy])
        def _(sx=sx, sy=sy):
            incoming_c(sx, sy).wait_recv()

    for m in range(M):
        for sy, at_col in enumerate((7, 8 + CJ)):
            for r in range(CI):
                dpad[m, r + 2, at_col : at_col + 1] = col_in[sy, m, r : r + 1]
            strip[m, sy, 2 : 2 + CI] = col_in[sy, m, 0:CI]
            for sx, r0 in enumerate((0, CI + 2)):
                strip[m, sy, r0 : r0 + 2] = cor_in[sx, sy, 2 * m : 2 * m + 2]
                for q in range(2):
                    dpad[m, r0 + q, at_col : at_col + 1] = cor_in[sx, sy, 2 * m + q : 2 * m + q + 1]

    inside_hi = (gx < GX - 1).astype(F32)
    for m in range(M):
        c, make_u, make_v, gain_j, loss = coefficients(m)
        for sx in range(2):
            @pl.when(has_x[sx])
            def _(sx=sx, m=m):
                incoming_x(sx, m).wait_recv()
        for q in range(2):
            dpad[m, q, 8 : 8 + CJ] = from_lo[m, 2 + q]
            dpad[m, CI + 2 + q, 8 : 8 + CJ] = from_hi[m, q]

        def full(r):
            if r < 0:
                return from_lo[m, CI + r]
            if r >= CI:
                return from_hi[m, r - CI]
            return d_ref[m, r]

        for r in range(-2, CI + 2):
            u = image(
                c, make_u, make_v, gain_j, loss, row_scalars(c, r),
                full(r - 2), full(r - 1), full(r), full(r + 1), full(r + 2),
                dpad[m, r + 2, 7 : 7 + CJ], dpad[m, r + 2, 9 : 9 + CJ],
            )
            if r >= CI:
                u = u * inside_hi
            upad[m, r + 2, 8 : 8 + CJ] = u

        i4 = (first_i + lax.broadcasted_iota(jnp.int32, (CI, NK), 0)).astype(F32)
        scalars = (
            c[1] * (i4 + 1.0),
            0.5 * c[4] * (i4 + 2.0) * (i4 + 1.0),
            c[1] * i4 + 0.5 * c[4] * i4 * (i4 - 1.0),
        )
        for sy, (jj, at_col) in enumerate(((-1, 7), (CJ, 8 + CJ))):
            j = jnp.full((1, NK), (first_j + jj).astype(F32))
            ratio = j / c[7]
            mu = c[0] / (1.0 + ratio * ratio)
            lo = mu + make_v + c[3] * j + (c[5] + c[6]) * k_row
            inner, outer = col_out[sy, m, 0:CI], col_in[sy, m, CI : 2 * CI]
            left, right = (outer, inner) if sy == 0 else (inner, outer)
            u = image(
                c, mu, make_v, c[3] * (j + 1.0), lo, scalars,
                strip[m, sy, 0:4], strip[m, sy, 1:5], strip[m, sy, 2:6], strip[m, sy, 3:7], strip[m, sy, 4:8],
                left, right,
            )
            if sy == 1:
                u = u * (gy < GY - 1).astype(F32)
            for r in range(CI):
                upad[m, r + 2, at_col : at_col + 1] = u[r : r + 1]

        sums = [jnp.zeros((8, NK), F32) for _ in PAIRS]
        for r in range(CI):
            mid = lambda q: upad[m, q + 2, 8 : 8 + CJ]
            u2 = image(
                c, make_u, make_v, gain_j, loss, row_scalars(c, r),
                mid(r - 2), mid(r - 1), mid(r), mid(r + 1), mid(r + 2),
                upad[m, r + 2, 7 : 7 + CJ], upad[m, r + 2, 9 : 9 + CJ],
            )
            out_ref[m, r] = u2
            basis = (d_ref[m, r], mid(r), u2)
            for p, (a, b) in enumerate(PAIRS):
                product = basis[a] * basis[b]
                sums[p] = sums[p] + product[0:8] + product[8:16]
        for p in range(len(PAIRS)):
            rows[p * M + m : p * M + m + 1] = jnp.sum(sums[p], axis=0, keepdims=True)

    n_rows = len(PAIRS) * M
    column = jnp.sum(rows[...], axis=1, keepdims=True)
    lanes = lax.broadcasted_iota(jnp.int32, (n_rows, NK), 1)
    places = lax.broadcasted_iota(jnp.int32, (n_rows, NK), 0)
    acc = jnp.sum(jnp.where(lanes == places, column, 0.0), axis=0, keepdims=True)

    total[0] = acc

    def early_copy(p):
        return pltpu.make_async_remote_copy(
            src_ref=total.at[0], dst_ref=direct.at[(gx - 4 * FAR_Z) * GY + gy], send_sem=e_send.at[0], recv_sem=e_recv.at[0],
            device_id=p, device_id_type=MESH,
        )

    @pl.when(far)
    def _():
        for p in EARLY:
            early_copy(p).start()

    def y_row(a):
        return pltpu.make_async_remote_copy(
            src_ref=total.at[0], dst_ref=slots_gy.at[a - 1], send_sem=r_send.at[0], recv_sem=r_recv.at[0],
            device_id=(gx, lax.rem(gy + a, GY)), device_id_type=MESH,
        )

    def x_row(a):
        return pltpu.make_async_remote_copy(
            src_ref=total.at[1], dst_ref=slots_gx.at[gx], send_sem=r_send.at[1], recv_sem=r_recv.at[1],
            device_id=(lax.rem(gx + a, GX), gy), device_id_type=MESH,
        )

    def awaited(rows_ref, send_sem, recv_sem):
        return pltpu.make_async_remote_copy(
            src_ref=rows_ref, dst_ref=rows_ref, send_sem=send_sem, recv_sem=recv_sem,
            device_id=(gx, lax.rem(gy + 1, GY)), device_id_type=MESH,
        )

    for a in STAGE_GY:
        y_row(a).start()
    y_rows = awaited(slots_gy, r_send.at[0], r_recv.at[0])
    y_rows.wait_recv()
    acc = acc + jnp.sum(slots_gy[...], axis=0)
    total[1] = acc
    slots_gx[gx] = acc

    def wanted(a):
        return jnp.logical_not(far & is_early(lax.rem(gx + a, GX), gy))

    pl.semaphore_wait(known.at[2], len(TOLD[2]))
    for a in STAGE_GX:
        @pl.when(wanted(a))
        def _(a=a):
            x_row(a).start()

    @pl.when(early)
    def _():
        awaited(slots_gx.at[0 : 4 * FAR_Z - 1], r_send.at[1], r_recv.at[1]).wait_recv()
        near_sum = jnp.sum(slots_gx[0 : 4 * FAR_Z], axis=0)
        awaited(direct, e_send.at[0], e_recv.at[0]).wait_recv()
        total[2] = near_sum + jnp.sum(direct[...], axis=0)

    @pl.when(jnp.logical_not(early))
    def _():
        awaited(slots_gx.at[0 : GX - 1], r_send.at[1], r_recv.at[1]).wait_recv()
        total[2] = jnp.sum(slots_gx[...], axis=0)

    acc = total[2]

    picked = [acc if p == 0 else roll_lanes(acc, -M * p) for p in range(len(PAIRS))]
    ok = lane < M
    picked = [jnp.where(ok, value, 1.0) for value in picked]
    scale = 1.0 / picked[0]
    a1, a2, b11, b12, b22 = [value * scale for value in picked[1:]]
    h00 = a1
    n1 = b11 - h00 * h00
    h10 = jnp.sqrt(n1)
    e = a2 - h00 * a1
    h01 = e / h10
    h11 = ((b12 - h00 * b11) - h00 * e) / n1
    ss = (b22 - h00 * b12) - h00 * (b12 - h00 * b11)
    h21 = jnp.sqrt(ss / n1 - h01 * h01 - h11 * h11)

    step_scale = lam_row * TAU
    entries = [step_scale * h for h in (h00, h10, h01, h11, h21)]
    small = 1.0 / 2.0**SQUARINGS
    g00, g10, g01, g11, g21 = [entry * small for entry in entries]
    one, zero = jnp.ones_like(h00), jnp.zeros_like(h00)
    p00, p01, p10, p11 = one, zero, zero, one
    w0 = w1 = zero
    for term in range(TAYLOR_TERMS, 0, -1):
        f = 1.0 / term
        w0, w1 = g21 * f * p10, g21 * f * p11
        q00 = 1.0 + (g00 * f * p00 + g01 * f * p10)
        q01 = g00 * f * p01 + g01 * f * p11
        q10 = g10 * f * p00 + g11 * f * p10
        q11 = 1.0 + (g10 * f * p01 + g11 * f * p11)
        p00, p01, p10, p11 = q00, q01, q10, q11
    for _ in range(SQUARINGS):
        w0, w1 = w0 + (w0 * p00 + w1 * p10), w1 + (w0 * p01 + w1 * p11)
        q00 = p00 * p00 + p01 * p10
        q01 = p00 * p01 + p01 * p11
        q10 = p10 * p00 + p11 * p10
        q11 = p10 * p01 + p11 * p11
        p00, p01, p10, p11 = q00, q01, q10, q11
    e0, e1, e2 = p00, p10, w0
    inv10 = 1.0 / h10
    e2 = e2 / h21
    f0 = e0 - e1 * h00 * inv10 + e2 * (h11 * h00 * inv10 - h01)
    f1 = (e1 - e2 * (h00 + h11)) * inv10
    f2 = e2 * inv10

    eye = lax.broadcasted_iota(jnp.int32, (8, NK), 0) == lax.broadcasted_iota(jnp.int32, (8, NK), 1)
    lanes8 = lax.broadcasted_iota(jnp.int32, (8, NK), 1)
    table = jnp.zeros((8, NK), F32)
    for q, entry in enumerate(entries):
        column = jnp.sum(jnp.where(eye, entry, 0.0), axis=1, keepdims=True)
        table = jnp.where(lanes8 == q, column, table)
    entry_ref[...] = table[:M, :5]

    for m in range(M):
        s0, s1, s2 = (jnp.broadcast_to(f[:, m : m + 1], (CJ, NK)) for f in (f0, f1, f2))
        for r in range(CI):
            out_ref[m, r] = s0 * d_ref[m, r] + s1 * upad[m, r + 2, 8 : 8 + CJ] + s2 * out_ref[m, r]

    y_rows.wait_send()

    @pl.when(far)
    def _():
        for p in EARLY:
            early_copy(p).wait_send()
        for a in STAGE_GX:
            @pl.when(wanted(a))
            def _(a=a):
                x_row(a).wait_send()

    @pl.when(jnp.logical_not(far))
    def _():
        awaited(slots_gx.at[0 : GX - 1], r_send.at[1], r_recv.at[1]).wait_send()

    for sy in range(2):
        @pl.when(has_y[sy])
        def _(sy=sy):
            y_copy(sy).wait_send()
    for sx, sy in itertools.product((0, 1), (0, 1)):
        @pl.when(has_x[sx] & has_y[sy])
        def _(sx=sx, sy=sy):
            c_copy(sx, sy).wait_send()
    for m in range(M):
        for sx in range(2):
            @pl.when(has_x[sx])
            def _(sx=sx, m=m):
                x_copy(sx, m).wait_send()


def store(field_ref, entry_ref, field_out, entry_out, sems):
    copies = [
        pltpu.make_async_copy(field_ref, field_out, sems.at[0]),
        pltpu.make_async_copy(entry_ref, entry_out, sems.at[1]),
    ]
    for copy in copies:
        copy.start()
    for copy in copies:
        copy.wait()


def shards(density, rate_table):
    vmem = functools.partial(pltpu.VMEM, dtype=F32)
    dma = pltpu.SemaphoreType.DMA
    results = pl.pallas_call(
        kernel,
        out_shape=(pltpu.VMEM(density.shape, F32), pltpu.VMEM((M, 5), F32)),
        in_specs=[pl.BlockSpec(memory_space=pl.ANY), pl.BlockSpec(memory_space=pl.ANY)],
        out_specs=(pl.BlockSpec(memory_space=pltpu.VMEM), pl.BlockSpec(memory_space=pltpu.VMEM)),
        scratch_shapes=[
            vmem((M, CI, CJ, NK)),
            pltpu.SMEM((M, 9), F32),
            vmem((M, CI + 4, 32, NK)),
            vmem((M, CI + 4, 32, NK)),
            vmem((M, CI, CJ, NK)),
            vmem((M, CI, CJ, NK)),
            vmem((2, M, 8, NK)),
            vmem((2, M, 8, NK)),
            vmem((2, 2, 8, NK)),
            vmem((2, 2, 8, NK)),
            vmem((M, 2, 8, NK)),
            vmem((len(PAIRS) * M, NK)),
            vmem((3, 1, NK)),
            vmem((GX, 1, NK)),
            vmem((GY - 1, 1, NK)),
            vmem((N_FAR, 1, NK)),
            dma((2, M)),
            dma((2, M)),
            dma((2,)),
            dma((2,)),
            dma((2, 2)),
            dma((2, 2)),
            dma((2,)),
            dma((2,)),
            dma((1,)),
            dma((1,)),
            dma((2,)),
            pltpu.SemaphoreType.REGULAR((3,)),
        ],
        compiler_params=pltpu.CompilerParams(collective_id=0, has_side_effects=True),
    )(density, rate_table)
    return pl.pallas_call(
        store,
        out_shape=(jax.ShapeDtypeStruct(density.shape, F32), jax.ShapeDtypeStruct((M, 5), F32)),
        in_specs=[pl.BlockSpec(memory_space=pltpu.VMEM)] * 2,
        out_specs=(pl.BlockSpec(memory_space=pl.ANY),) * 2,
        scratch_shapes=[dma((2,))],
        compiler_params=pltpu.CompilerParams(vmem_limit_bytes=1 << 20),
    )(*results)


def solution(mesh):
    specs = (P(None, "gx", "gy", None), P())
    return jax.shard_map(shards, mesh=mesh, in_specs=specs, out_specs=specs, check_vma=False)
```

```python
import functools
import itertools

import jax
import jax.numpy as jnp
from jax import lax
from jax.experimental import pallas as pl
from jax.experimental.pallas import tpu as pltpu
from jax.sharding import PartitionSpec as P

MESH = pl.DeviceIdType.MESH
F32 = jnp.float32
TAU = 0.01
TAYLOR_TERMS = 16
SQUARINGS = 4
M, CI, CJ, NK = 4, 4, 16, 128
NI, NJ = 128, 256
GX, GY = 32, 16
PAIRS = ((0, 0), (0, 1), (0, 2), (1, 1), (1, 2), (2, 2))


def ring(size):
    return sorted(range(1, size), key=lambda a: -min(a, size - a))


def hops_gx(a):
    z, x = a // 4, a % 4
    return min(z, 8 - z) + min(x, 4 - x)


STAGE_GX = sorted(range(1, GX), key=lambda a: -hops_gx(a))
STAGE_GY = ring(GY)

GREETED = (
    [(0, dx, 0, 0) for dx in (1, 3)]
    + [(0, 0, dy, c) for dy in (1, 7) for c in (1, 0)]
    + [(dz, 0, 0, 0) for dz in (1, 7)]
    + [(0, 0, 0, 1)]
)
TOLD = (
    GREETED,
    [(dz, 0, 0, 0) for dz in (2, 6, 1, 7)] + [(0, 0, dy, 0) for dy in (2, 6)],
    [(dz, 0, 0, 0) for dz in (2, 6)],
)


FAR_Z = 4
N_FAR = (GX - 4 * FAR_Z) * GY
EARLY_REACH = 10


def is_early(gx, gy):
    z, x, y = gx // 4, gx % 4, gy // 2
    return (5 * y + 2 * x + 4 * z <= EARLY_REACH) & (gx + gy > 0)


EARLY = sorted(
    (p for p in itertools.product(range(GX), range(GY)) if is_early(*p)),
    key=lambda p: 5 * (p[1] // 2) + 2 * (p[0] % 4) + 4 * (p[0] // 4),
)
FAR = sorted(
    itertools.product(range(4 * FAR_Z, GX), range(GY)),
    key=lambda p: (abs(p[1] // 2 - 4), abs(p[0] % 4 - 2), p),
)


def row_sum(value):
    return jnp.sum(value, axis=0, keepdims=True)


def roll_lanes(value, shift):
    return pltpu.roll(value, shift % NK, value.ndim - 1)


def kernel(
    d_hbm, rate_hbm, out_ref, entry_ref,
    d_ref, rate_ref, dpad, upad, from_lo, from_hi, col_out, col_in, cor_out, cor_in, strip,
    rows, total, slots_gx, slots_gy, direct,
    x_send, x_recv, y_send, y_recv, c_send, c_recv, r_send, r_recv, e_send, e_recv, load, known,
):
    gx, gy = lax.axis_index("gx"), lax.axis_index("gy")
    z, x, y, core = lax.div(gx, 4), lax.rem(gx, 4), lax.div(gy, 2), lax.rem(gy, 2)
    first_i, first_j = gx * CI, gy * CJ
    has_x = (gx > 0, gx < GX - 1)
    has_y = (gy > 0, gy < GY - 1)
    step = (-1, 1)
    has_edge = ((x == 0) & has_x[0], (x == 3) & has_x[1])

    def at(dx, dy):
        return (gx + dx, gy + dy)

    def offset(dz, dx, dy, dc):
        return (
            lax.rem(z + dz, GX // 4) * 4 + lax.rem(x + dx, 4),
            lax.rem(y + dy, GY // 2) * 2 + lax.rem(core + dc, 2),
        )

    barrier = pltpu.get_barrier_semaphore()
    for o in GREETED[:2]:
        pl.semaphore_signal(barrier, inc=1, device_id=offset(*o), device_id_type=MESH)
    for sx in range(2):
        @pl.when(has_edge[sx])
        def _(sx=sx):
            pl.semaphore_signal(barrier, inc=1, device_id=at(step[sx], 0), device_id_type=MESH)
    for sx, sy in itertools.product((0, 1), (0, 1)):
        @pl.when(has_x[sx] & has_y[sy])
        def _(sx=sx, sy=sy):
            pl.semaphore_signal(barrier, inc=1, device_id=at(step[sx], step[sy]), device_id_type=MESH)
    for o in GREETED[2:]:
        pl.semaphore_signal(barrier, inc=1, device_id=offset(*o), device_id_type=MESH)

    far, early = z >= FAR_Z, is_early(gx, gy)

    @pl.when(early)
    def _():
        for p in FAR:
            pl.semaphore_signal(barrier, inc=1, device_id=p, device_id_type=MESH)

    loads = [
        pltpu.make_async_copy(d_hbm, d_ref, load.at[0]),
        pltpu.make_async_copy(rate_hbm, rate_ref, load.at[1]),
    ]
    for copy in loads:
        copy.start()
    for copy in loads:
        copy.wait()

    for sy, (near, next_near) in enumerate(((0, 1), (CJ - 1, CJ - 2))):
        for m in range(M):
            for r in range(CI):
                col_out[sy, m, r : r + 1] = d_ref[m, r, near : near + 1]
                col_out[sy, m, CI + r : CI + r + 1] = d_ref[m, r, next_near : next_near + 1]
            for sx, r0 in enumerate((0, CI - 2)):
                for q in range(2):
                    cor_out[sx, sy, 2 * m + q : 2 * m + q + 1] = d_ref[m, r0 + q, near : near + 1]

    n_edge = has_edge[0].astype(jnp.int32) + has_edge[1].astype(jnp.int32)
    n_x = has_x[0].astype(jnp.int32) + has_x[1].astype(jnp.int32)
    n_y = has_y[0].astype(jnp.int32) + has_y[1].astype(jnp.int32)
    pl.semaphore_wait(barrier, len(GREETED) + n_edge + n_x * n_y + far.astype(jnp.int32) * len(EARLY))

    def x_copy(sx, m):
        dst = (from_hi, from_lo)[sx]
        return pltpu.make_async_remote_copy(
            src_ref=d_ref.at[m], dst_ref=dst.at[m], send_sem=x_send.at[sx, m], recv_sem=x_recv.at[1 - sx, m],
            device_id=at(step[sx], 0), device_id_type=MESH,
        )

    def y_copy(sy):
        return pltpu.make_async_remote_copy(
            src_ref=col_out.at[sy], dst_ref=col_in.at[1 - sy], send_sem=y_send.at[sy], recv_sem=y_recv.at[1 - sy],
            device_id=at(0, step[sy]), device_id_type=MESH,
        )

    def c_copy(sx, sy):
        return pltpu.make_async_remote_copy(
            src_ref=cor_out.at[sx, sy], dst_ref=cor_in.at[1 - sx, 1 - sy],
            send_sem=c_send.at[sx, sy], recv_sem=c_recv.at[1 - sx, 1 - sy],
            device_id=at(step[sx], step[sy]), device_id_type=MESH,
        )

    def incoming_x(sx, m):
        dst = (from_lo, from_hi)[sx]
        return pltpu.make_async_remote_copy(
            src_ref=d_ref.at[m], dst_ref=dst.at[m], send_sem=x_send.at[sx, m], recv_sem=x_recv.at[sx, m],
            device_id=at(step[sx], 0), device_id_type=MESH,
        )

    def incoming_y(sy):
        return pltpu.make_async_remote_copy(
            src_ref=col_out.at[sy], dst_ref=col_in.at[sy], send_sem=y_send.at[sy], recv_sem=y_recv.at[sy],
            device_id=at(0, step[sy]), device_id_type=MESH,
        )

    def incoming_c(sx, sy):
        return pltpu.make_async_remote_copy(
            src_ref=cor_out.at[sx, sy], dst_ref=cor_in.at[sx, sy],
            send_sem=c_send.at[sx, sy], recv_sem=c_recv.at[sx, sy],
            device_id=at(step[sx], step[sy]), device_id_type=MESH,
        )

    def start_x(m):
        for sx in range(2):
            @pl.when(has_x[sx])
            def _(sx=sx):
                x_copy(sx, m).start()

    start_x(0)
    for sy in range(2):
        @pl.when(has_y[sy])
        def _(sy=sy):
            y_copy(sy).start()
    for sx, sy in itertools.product((0, 1), (0, 1)):
        @pl.when(has_x[sx] & has_y[sy])
        def _(sx=sx, sy=sy):
            c_copy(sx, sy).start()
    for m in range(1, M):
        start_x(m)

    def tell(level):
        for o in TOLD[level]:
            pl.semaphore_signal(known.at[level], inc=1, device_id=offset(*o), device_id_type=MESH)

    tell(0)

    lane = lax.broadcasted_iota(jnp.int32, (1, NK), 1)
    k_row = lane.astype(F32)
    not_first = (lane > 0).astype(F32)
    j_col = (first_j + lax.broadcasted_iota(jnp.int32, (CJ, NK), 0)).astype(F32)
    lam_row = jnp.ones((1, NK), F32)
    rates = []
    for m in range(M):
        c = [rate_ref[m, r] for r in range(9)]
        lam = c[0] + 127.0 * c[1] + c[2] + 255.0 * c[3] + 8001.0 * c[4] + 127.0 * (c[5] + c[6])
        lam_row = jnp.where(lane == m, lam, lam_row)
        rates.append(c)
    inv_row = 1.0 / lam_row

    def coefficients(m):
        inv = inv_row[0, m]
        c = [rates[m][r] * inv for r in range(7)] + rates[m][7:]
        ratio_j = j_col / c[7]
        ratio_k = k_row / c[8]
        make_u = c[0] / (1.0 + ratio_j * ratio_j)
        make_v = c[2] / (1.0 + ratio_k * ratio_k)
        gain_j = c[3] * (j_col + 1.0)
        loss = make_u + make_v + c[3] * j_col + (c[5] + c[6]) * k_row
        return c, make_u, make_v, gain_j, loss

    def row_scalars(c, r):
        i = (first_i + r).astype(F32)
        down = c[1] * (i + 1.0)
        pair = 0.5 * c[4] * (i + 2.0) * (i + 1.0)
        out = c[1] * i + 0.5 * c[4] * i * (i - 1.0)
        return down, pair, out

    def image(c, make_u, make_v, gain_j, loss, scalars, before2, before, here, after, after2, left, right):
        down, pair, out = scalars
        result = make_u * before + down * after + make_v * left + gain_j * right
        result = result + roll_lanes(after2, 1) * (pair * not_first)
        result = result + roll_lanes((c[5] * before2 + c[6] * here) * k_row, -1)
        return result - (loss + out) * here

    for sx in range(2):
        @pl.when(jnp.logical_not(has_x[sx]))
        def _(sx=sx):
            (from_lo, from_hi)[sx][...] = jnp.zeros_like(from_lo)
    for sy in range(2):
        @pl.when(jnp.logical_not(has_y[sy]))
        def _(sy=sy):
            col_in[sy] = jnp.zeros_like(col_in[sy])
    for sx, sy in itertools.product((0, 1), (0, 1)):
        @pl.when(jnp.logical_not(has_x[sx] & has_y[sy]))
        def _(sx=sx, sy=sy):
            cor_in[sx, sy] = jnp.zeros_like(cor_in[sx, sy])

    for m in range(M):
        for r in range(CI):
            dpad[m, r + 2, 8 : 8 + CJ] = d_ref[m, r]

    pl.semaphore_wait(known.at[0], len(TOLD[0]))
    tell(1)

    for sy in range(2):
        @pl.when(has_y[sy])
        def _(sy=sy):
            incoming_y(sy).wait_recv()
    for sx, sy in itertools.product((0, 1), (0, 1)):
        @pl.when(has_x[sx] & has_y[sy])
        def _(sx=sx, sy=sy):
            incoming_c(sx, sy).wait_recv()

    for m in range(M):
        for sy, at_col in enumerate((7, 8 + CJ)):
            for r in range(CI):
                dpad[m, r + 2, at_col : at_col + 1] = col_in[sy, m, r : r + 1]
            strip[m, sy, 2 : 2 + CI] = col_in[sy, m, 0:CI]
            for sx, r0 in enumerate((0, CI + 2)):
                strip[m, sy, r0 : r0 + 2] = cor_in[sx, sy, 2 * m : 2 * m + 2]
                for q in range(2):
                    dpad[m, r0 + q, at_col : at_col + 1] = cor_in[sx, sy, 2 * m + q : 2 * m + q + 1]

    inside_hi = (gx < GX - 1).astype(F32)
    for m in range(M):
        c, make_u, make_v, gain_j, loss = coefficients(m)
        for sx in range(2):
            @pl.when(has_x[sx])
            def _(sx=sx, m=m):
                incoming_x(sx, m).wait_recv()
        for q in range(2):
            dpad[m, q, 8 : 8 + CJ] = from_lo[m, 2 + q]
            dpad[m, CI + 2 + q, 8 : 8 + CJ] = from_hi[m, q]

        def full(r):
            if r < 0:
                return from_lo[m, CI + r]
            if r >= CI:
                return from_hi[m, r - CI]
            return d_ref[m, r]

        for r in range(-2, CI + 2):
            u = image(
                c, make_u, make_v, gain_j, loss, row_scalars(c, r),
                full(r - 2), full(r - 1), full(r), full(r + 1), full(r + 2),
                dpad[m, r + 2, 7 : 7 + CJ], dpad[m, r + 2, 9 : 9 + CJ],
            )
            if r >= CI:
                u = u * inside_hi
            upad[m, r + 2, 8 : 8 + CJ] = u

        i4 = (first_i + lax.broadcasted_iota(jnp.int32, (CI, NK), 0)).astype(F32)
        scalars = (
            c[1] * (i4 + 1.0),
            0.5 * c[4] * (i4 + 2.0) * (i4 + 1.0),
            c[1] * i4 + 0.5 * c[4] * i4 * (i4 - 1.0),
        )
        for sy, (jj, at_col) in enumerate(((-1, 7), (CJ, 8 + CJ))):
            j = jnp.full((1, NK), (first_j + jj).astype(F32))
            ratio = j / c[7]
            mu = c[0] / (1.0 + ratio * ratio)
            lo = mu + make_v + c[3] * j + (c[5] + c[6]) * k_row
            inner, outer = col_out[sy, m, 0:CI], col_in[sy, m, CI : 2 * CI]
            left, right = (outer, inner) if sy == 0 else (inner, outer)
            u = image(
                c, mu, make_v, c[3] * (j + 1.0), lo, scalars,
                strip[m, sy, 0:4], strip[m, sy, 1:5], strip[m, sy, 2:6], strip[m, sy, 3:7], strip[m, sy, 4:8],
                left, right,
            )
            if sy == 1:
                u = u * (gy < GY - 1).astype(F32)
            for r in range(CI):
                upad[m, r + 2, at_col : at_col + 1] = u[r : r + 1]

        sums = [jnp.zeros((8, NK), F32) for _ in PAIRS]
        for r in range(CI):
            mid = lambda q: upad[m, q + 2, 8 : 8 + CJ]
            u2 = image(
                c, make_u, make_v, gain_j, loss, row_scalars(c, r),
                mid(r - 2), mid(r - 1), mid(r), mid(r + 1), mid(r + 2),
                upad[m, r + 2, 7 : 7 + CJ], upad[m, r + 2, 9 : 9 + CJ],
            )
            out_ref[m, r] = u2
            basis = (d_ref[m, r], mid(r), u2)
            for p, (a, b) in enumerate(PAIRS):
                product = basis[a] * basis[b]
                sums[p] = sums[p] + product[0:8] + product[8:16]
        for p in range(len(PAIRS)):
            rows[p * M + m : p * M + m + 1] = jnp.sum(sums[p], axis=0, keepdims=True)

    n_rows = len(PAIRS) * M
    column = jnp.sum(rows[...], axis=1, keepdims=True)
    lanes = lax.broadcasted_iota(jnp.int32, (n_rows, NK), 1)
    places = lax.broadcasted_iota(jnp.int32, (n_rows, NK), 0)
    acc = jnp.sum(jnp.where(lanes == places, column, 0.0), axis=0, keepdims=True)

    total[0] = acc

    def early_copy(p):
        return pltpu.make_async_remote_copy(
            src_ref=total.at[0], dst_ref=direct.at[pl.ds((gx - 4 * FAR_Z) * GY + gy, 1)], send_sem=e_send.at[0], recv_sem=e_recv.at[0],
            device_id=p, device_id_type=MESH,
        )

    @pl.when(far)
    def _():
        for p in EARLY:
            early_copy(p).start()

    def y_row(a):
        return pltpu.make_async_remote_copy(
            src_ref=total.at[0], dst_ref=slots_gy.at[pl.ds(gy, 1)], send_sem=r_send.at[0], recv_sem=r_recv.at[0],
            device_id=(gx, lax.rem(gy + a, GY)), device_id_type=MESH,
        )

    def x_row(a):
        return pltpu.make_async_remote_copy(
            src_ref=total.at[1], dst_ref=slots_gx.at[pl.ds(gx, 1)], send_sem=r_send.at[1], recv_sem=r_recv.at[1],
            device_id=(lax.rem(gx + a, GX), gy), device_id_type=MESH,
        )

    def awaited(rows_ref, send_sem, recv_sem):
        return pltpu.make_async_remote_copy(
            src_ref=rows_ref, dst_ref=rows_ref, send_sem=send_sem, recv_sem=recv_sem,
            device_id=(gx, lax.rem(gy + 1, GY)), device_id_type=MESH,
        )

    pl.semaphore_wait(known.at[1], len(TOLD[1]))
    tell(2)
    for a in STAGE_GY:
        y_row(a).start()
    slots_gy[pl.ds(gy, 1)] = acc
    y_rows = awaited(slots_gy.at[0 : GY - 1], r_send.at[0], r_recv.at[0])
    y_rows.wait_recv()
    acc = row_sum(slots_gy[...])
    total[1] = acc
    slots_gx[pl.ds(gx, 1)] = acc

    def wanted(a):
        return jnp.logical_not(far & is_early(lax.rem(gx + a, GX), gy))

    pl.semaphore_wait(known.at[2], len(TOLD[2]))
    for a in STAGE_GX:
        @pl.when(wanted(a))
        def _(a=a):
            x_row(a).start()

    @pl.when(early)
    def _():
        awaited(slots_gx.at[0 : 4 * FAR_Z - 1], r_send.at[1], r_recv.at[1]).wait_recv()
        near_sum = row_sum(slots_gx[0 : 4 * FAR_Z])
        awaited(direct, e_send.at[0], e_recv.at[0]).wait_recv()
        total[2] = near_sum + row_sum(direct[...])

    @pl.when(jnp.logical_not(early))
    def _():
        awaited(slots_gx.at[0 : GX - 1], r_send.at[1], r_recv.at[1]).wait_recv()
        total[2] = row_sum(slots_gx[...])

    acc = total[2]

    picked = [acc if p == 0 else roll_lanes(acc, -M * p) for p in range(len(PAIRS))]
    ok = lane < M
    picked = [jnp.where(ok, value, 1.0) for value in picked]
    scale = 1.0 / picked[0]
    a1, a2, b11, b12, b22 = [value * scale for value in picked[1:]]
    h00 = a1
    n1 = b11 - h00 * h00
    h10 = jnp.sqrt(n1)
    e = a2 - h00 * a1
    h01 = e / h10
    h11 = ((b12 - h00 * b11) - h00 * e) / n1
    ss = (b22 - h00 * b12) - h00 * (b12 - h00 * b11)
    h21 = jnp.sqrt(ss / n1 - h01 * h01 - h11 * h11)

    step_scale = lam_row * TAU
    entries = [step_scale * h for h in (h00, h10, h01, h11, h21)]
    small = 1.0 / 2.0**SQUARINGS
    g00, g10, g01, g11, g21 = [entry * small for entry in entries]
    one, zero = jnp.ones_like(h00), jnp.zeros_like(h00)
    p00, p01, p10, p11 = one, zero, zero, one
    w0 = w1 = zero
    for term in range(TAYLOR_TERMS, 0, -1):
        f = 1.0 / term
        w0, w1 = g21 * f * p10, g21 * f * p11
        q00 = 1.0 + (g00 * f * p00 + g01 * f * p10)
        q01 = g00 * f * p01 + g01 * f * p11
        q10 = g10 * f * p00 + g11 * f * p10
        q11 = 1.0 + (g10 * f * p01 + g11 * f * p11)
        p00, p01, p10, p11 = q00, q01, q10, q11
    for _ in range(SQUARINGS):
        w0, w1 = w0 + (w0 * p00 + w1 * p10), w1 + (w0 * p01 + w1 * p11)
        q00 = p00 * p00 + p01 * p10
        q01 = p00 * p01 + p01 * p11
        q10 = p10 * p00 + p11 * p10
        q11 = p10 * p01 + p11 * p11
        p00, p01, p10, p11 = q00, q01, q10, q11
    e0, e1, e2 = p00, p10, w0
    inv10 = 1.0 / h10
    e2 = e2 / h21
    f0 = e0 - e1 * h00 * inv10 + e2 * (h11 * h00 * inv10 - h01)
    f1 = (e1 - e2 * (h00 + h11)) * inv10
    f2 = e2 * inv10

    eye = lax.broadcasted_iota(jnp.int32, (8, NK), 0) == lax.broadcasted_iota(jnp.int32, (8, NK), 1)
    lanes8 = lax.broadcasted_iota(jnp.int32, (8, NK), 1)
    table = jnp.zeros((8, NK), F32)
    for q, entry in enumerate(entries):
        column = jnp.sum(jnp.where(eye, entry, 0.0), axis=1, keepdims=True)
        table = jnp.where(lanes8 == q, column, table)
    entry_ref[...] = table[:M, :5]

    for m in range(M):
        s0, s1, s2 = (jnp.broadcast_to(f[:, m : m + 1], (CJ, NK)) for f in (f0, f1, f2))
        for r in range(CI):
            out_ref[m, r] = s0 * d_ref[m, r] + s1 * upad[m, r + 2, 8 : 8 + CJ] + s2 * out_ref[m, r]

    y_rows.wait_send()

    @pl.when(far)
    def _():
        for p in EARLY:
            early_copy(p).wait_send()
        for a in STAGE_GX:
            @pl.when(wanted(a))
            def _(a=a):
                x_row(a).wait_send()

    @pl.when(jnp.logical_not(far))
    def _():
        awaited(slots_gx.at[0 : GX - 1], r_send.at[1], r_recv.at[1]).wait_send()

    for sy in range(2):
        @pl.when(has_y[sy])
        def _(sy=sy):
            y_copy(sy).wait_send()
    for sx, sy in itertools.product((0, 1), (0, 1)):
        @pl.when(has_x[sx] & has_y[sy])
        def _(sx=sx, sy=sy):
            c_copy(sx, sy).wait_send()
    for m in range(M):
        for sx in range(2):
            @pl.when(has_x[sx])
            def _(sx=sx, m=m):
                x_copy(sx, m).wait_send()


def store(field_ref, entry_ref, field_out, entry_out, sems):
    copies = [
        pltpu.make_async_copy(field_ref, field_out, sems.at[0]),
        pltpu.make_async_copy(entry_ref, entry_out, sems.at[1]),
    ]
    for copy in copies:
        copy.start()
    for copy in copies:
        copy.wait()


def shards(density, rate_table):
    vmem = functools.partial(pltpu.VMEM, dtype=F32)
    dma = pltpu.SemaphoreType.DMA
    results = pl.pallas_call(
        kernel,
        out_shape=(pltpu.VMEM(density.shape, F32), pltpu.VMEM((M, 5), F32)),
        in_specs=[pl.BlockSpec(memory_space=pl.ANY), pl.BlockSpec(memory_space=pl.ANY)],
        out_specs=(pl.BlockSpec(memory_space=pltpu.VMEM), pl.BlockSpec(memory_space=pltpu.VMEM)),
        scratch_shapes=[
            vmem((M, CI, CJ, NK)),
            pltpu.SMEM((M, 9), F32),
            vmem((M, CI + 4, 32, NK)),
            vmem((M, CI + 4, 32, NK)),
            vmem((M, CI, CJ, NK)),
            vmem((M, CI, CJ, NK)),
            vmem((2, M, 8, NK)),
            vmem((2, M, 8, NK)),
            vmem((2, 2, 8, NK)),
            vmem((2, 2, 8, NK)),
            vmem((M, 2, 8, NK)),
            vmem((len(PAIRS) * M, NK)),
            vmem((3, 1, NK)),
            vmem((GX, NK)),
            vmem((GY, NK)),
            vmem((N_FAR, NK)),
            dma((2, M)),
            dma((2, M)),
            dma((2,)),
            dma((2,)),
            dma((2, 2)),
            dma((2, 2)),
            dma((2,)),
            dma((2,)),
            dma((1,)),
            dma((1,)),
            dma((2,)),
            pltpu.SemaphoreType.REGULAR((3,)),
        ],
        compiler_params=pltpu.CompilerParams(collective_id=0, has_side_effects=True),
    )(density, rate_table)
    return pl.pallas_call(
        store,
        out_shape=(jax.ShapeDtypeStruct(density.shape, F32), jax.ShapeDtypeStruct((M, 5), F32)),
        in_specs=[pl.BlockSpec(memory_space=pltpu.VMEM)] * 2,
        out_specs=(pl.BlockSpec(memory_space=pl.ANY),) * 2,
        scratch_shapes=[dma((2,))],
        compiler_params=pltpu.CompilerParams(vmem_limit_bytes=1 << 20),
    )(*results)


def solution(mesh):
    specs = (P(None, "gx", "gy", None), P())
    return jax.shard_map(shards, mesh=mesh, in_specs=specs, out_specs=specs, check_vma=False)
```

```python
import functools
import itertools

import jax
import jax.numpy as jnp
from jax import lax
from jax.experimental import pallas as pl
from jax.experimental.pallas import tpu as pltpu
from jax.sharding import PartitionSpec as P

MESH = pl.DeviceIdType.MESH
F32 = jnp.float32
TAU = 0.01
TINY = 1e-36
TAYLOR_TERMS = 16
SQUARINGS = 4
M, CI, CJ, NK = 4, 4, 16, 128
NI, NJ = 128, 256
GX, GY = 32, 16
PAIRS = ((0, 0), (0, 1), (0, 2), (1, 1), (1, 2), (2, 2))


def ring(size):
    return sorted(range(1, size), key=lambda a: -min(a, size - a))


def hops_gx(a):
    z, x = a // 4, a % 4
    return min(z, 8 - z) + min(x, 4 - x)


STAGE_GX = sorted(range(1, GX), key=lambda a: -hops_gx(a))
STAGE_GY = ring(GY)

GREETED = (
    [(0, dx, 0, 0) for dx in (1, 3)]
    + [(0, 0, dy, c) for dy in (1, 7) for c in (1, 0)]
    + [(dz, 0, 0, 0) for dz in (1, 7)]
    + [(0, 0, 0, 1)]
)
TOLD = (
    GREETED,
    [(dz, 0, 0, 0) for dz in (2, 6, 1, 7)] + [(0, 0, dy, 0) for dy in (2, 6)],
    [(dz, 0, 0, 0) for dz in (2, 6)],
)


FAR_Z = 4
N_FAR = (GX - 4 * FAR_Z) * GY
EARLY_REACH = 10


def is_early(gx, gy):
    z, x, y = gx // 4, gx % 4, gy // 2
    return (5 * y + 2 * x + 4 * z <= EARLY_REACH) & (gx + gy > 0)


EARLY = sorted(
    (p for p in itertools.product(range(GX), range(GY)) if is_early(*p)),
    key=lambda p: 5 * (p[1] // 2) + 2 * (p[0] % 4) + 4 * (p[0] // 4),
)
FAR = sorted(
    itertools.product(range(4 * FAR_Z, GX), range(GY)),
    key=lambda p: (abs(p[1] // 2 - 4), abs(p[0] % 4 - 2), p),
)


def row_sum(value):
    return jnp.sum(value, axis=0, keepdims=True)


def roll_lanes(value, shift):
    return pltpu.roll(value, shift % NK, value.ndim - 1)


def kernel(
    d_hbm, rate_hbm, out_ref, entry_ref,
    d_ref, rate_ref, dpad, upad, from_lo, from_hi, col_out, col_in, cor_out, cor_in, strip,
    rows, total, slots_gx, slots_gy, direct,
    x_send, x_recv, y_send, y_recv, c_send, c_recv, r_send, r_recv, e_send, e_recv, load, known,
):
    gx, gy = lax.axis_index("gx"), lax.axis_index("gy")
    z, x, y, core = lax.div(gx, 4), lax.rem(gx, 4), lax.div(gy, 2), lax.rem(gy, 2)
    first_i, first_j = gx * CI, gy * CJ
    has_x = (gx > 0, gx < GX - 1)
    has_y = (gy > 0, gy < GY - 1)
    step = (-1, 1)
    has_edge = ((x == 0) & has_x[0], (x == 3) & has_x[1])

    def at(dx, dy):
        return (gx + dx, gy + dy)

    def offset(dz, dx, dy, dc):
        return (
            lax.rem(z + dz, GX // 4) * 4 + lax.rem(x + dx, 4),
            lax.rem(y + dy, GY // 2) * 2 + lax.rem(core + dc, 2),
        )

    barrier = pltpu.get_barrier_semaphore()
    for o in GREETED[:2]:
        pl.semaphore_signal(barrier, inc=1, device_id=offset(*o), device_id_type=MESH)
    for sx in range(2):
        @pl.when(has_edge[sx])
        def _(sx=sx):
            pl.semaphore_signal(barrier, inc=1, device_id=at(step[sx], 0), device_id_type=MESH)
    for sx, sy in itertools.product((0, 1), (0, 1)):
        @pl.when(has_x[sx] & has_y[sy])
        def _(sx=sx, sy=sy):
            pl.semaphore_signal(barrier, inc=1, device_id=at(step[sx], step[sy]), device_id_type=MESH)
    for o in GREETED[2:]:
        pl.semaphore_signal(barrier, inc=1, device_id=offset(*o), device_id_type=MESH)

    far, early = z >= FAR_Z, is_early(gx, gy)

    @pl.when(early)
    def _():
        for p in FAR:
            pl.semaphore_signal(barrier, inc=1, device_id=p, device_id_type=MESH)

    loads = [
        pltpu.make_async_copy(d_hbm, d_ref, load.at[0]),
        pltpu.make_async_copy(rate_hbm, rate_ref, load.at[1]),
    ]
    for copy in loads:
        copy.start()
    for copy in loads:
        copy.wait()

    for sy, (near, next_near) in enumerate(((0, 1), (CJ - 1, CJ - 2))):
        for m in range(M):
            for r in range(CI):
                col_out[sy, m, r : r + 1] = d_ref[m, r, near : near + 1]
                col_out[sy, m, CI + r : CI + r + 1] = d_ref[m, r, next_near : next_near + 1]
            for sx, r0 in enumerate((0, CI - 2)):
                for q in range(2):
                    cor_out[sx, sy, 2 * m + q : 2 * m + q + 1] = d_ref[m, r0 + q, near : near + 1]

    n_edge = has_edge[0].astype(jnp.int32) + has_edge[1].astype(jnp.int32)
    n_x = has_x[0].astype(jnp.int32) + has_x[1].astype(jnp.int32)
    n_y = has_y[0].astype(jnp.int32) + has_y[1].astype(jnp.int32)
    pl.semaphore_wait(barrier, len(GREETED) + n_edge + n_x * n_y + far.astype(jnp.int32) * len(EARLY))

    def x_copy(sx, m):
        dst = (from_hi, from_lo)[sx]
        return pltpu.make_async_remote_copy(
            src_ref=d_ref.at[m], dst_ref=dst.at[m], send_sem=x_send.at[sx, m], recv_sem=x_recv.at[1 - sx, m],
            device_id=at(step[sx], 0), device_id_type=MESH,
        )

    def y_copy(sy):
        return pltpu.make_async_remote_copy(
            src_ref=col_out.at[sy], dst_ref=col_in.at[1 - sy], send_sem=y_send.at[sy], recv_sem=y_recv.at[1 - sy],
            device_id=at(0, step[sy]), device_id_type=MESH,
        )

    def c_copy(sx, sy):
        return pltpu.make_async_remote_copy(
            src_ref=cor_out.at[sx, sy], dst_ref=cor_in.at[1 - sx, 1 - sy],
            send_sem=c_send.at[sx, sy], recv_sem=c_recv.at[1 - sx, 1 - sy],
            device_id=at(step[sx], step[sy]), device_id_type=MESH,
        )

    def incoming_x(sx, m):
        dst = (from_lo, from_hi)[sx]
        return pltpu.make_async_remote_copy(
            src_ref=d_ref.at[m], dst_ref=dst.at[m], send_sem=x_send.at[sx, m], recv_sem=x_recv.at[sx, m],
            device_id=at(step[sx], 0), device_id_type=MESH,
        )

    def incoming_y(sy):
        return pltpu.make_async_remote_copy(
            src_ref=col_out.at[sy], dst_ref=col_in.at[sy], send_sem=y_send.at[sy], recv_sem=y_recv.at[sy],
            device_id=at(0, step[sy]), device_id_type=MESH,
        )

    def incoming_c(sx, sy):
        return pltpu.make_async_remote_copy(
            src_ref=cor_out.at[sx, sy], dst_ref=cor_in.at[sx, sy],
            send_sem=c_send.at[sx, sy], recv_sem=c_recv.at[sx, sy],
            device_id=at(step[sx], step[sy]), device_id_type=MESH,
        )

    def start_x(m):
        for sx in range(2):
            @pl.when(has_x[sx])
            def _(sx=sx):
                x_copy(sx, m).start()

    start_x(0)
    for sy in range(2):
        @pl.when(has_y[sy])
        def _(sy=sy):
            y_copy(sy).start()
    for sx, sy in itertools.product((0, 1), (0, 1)):
        @pl.when(has_x[sx] & has_y[sy])
        def _(sx=sx, sy=sy):
            c_copy(sx, sy).start()
    for m in range(1, M):
        start_x(m)

    def tell(level):
        for o in TOLD[level]:
            pl.semaphore_signal(known.at[level], inc=1, device_id=offset(*o), device_id_type=MESH)

    tell(0)

    lane = lax.broadcasted_iota(jnp.int32, (1, NK), 1)
    k_row = lane.astype(F32)
    not_first = (lane > 0).astype(F32)
    j_col = (first_j + lax.broadcasted_iota(jnp.int32, (CJ, NK), 0)).astype(F32)
    lam_row = jnp.ones((1, NK), F32)
    rates = []
    for m in range(M):
        c = [rate_ref[m, r] for r in range(9)]
        lam = c[0] + 127.0 * c[1] + c[2] + 255.0 * c[3] + 8001.0 * c[4] + 127.0 * (c[5] + c[6])
        lam_row = jnp.where(lane == m, lam, lam_row)
        rates.append(c)
    inv_row = 1.0 / lam_row

    def coefficients(m):
        inv = inv_row[0, m]
        c = [rates[m][r] * inv for r in range(7)] + rates[m][7:]
        ratio_j = j_col / c[7]
        ratio_k = k_row / c[8]
        make_u = c[0] / (1.0 + ratio_j * ratio_j)
        make_v = c[2] / (1.0 + ratio_k * ratio_k)
        gain_j = c[3] * (j_col + 1.0)
        loss = make_u + make_v + c[3] * j_col + (c[5] + c[6]) * k_row
        return c, make_u, make_v, gain_j, loss

    def row_scalars(c, r):
        i = (first_i + r).astype(F32)
        down = c[1] * (i + 1.0)
        pair = 0.5 * c[4] * (i + 2.0) * (i + 1.0)
        out = c[1] * i + 0.5 * c[4] * i * (i - 1.0)
        return down, pair, out

    def image(c, make_u, make_v, gain_j, loss, scalars, before2, before, here, after, after2, left, right):
        down, pair, out = scalars
        result = make_u * before + down * after + make_v * left + gain_j * right
        result = result + roll_lanes(after2, 1) * (pair * not_first)
        result = result + roll_lanes((c[5] * before2 + c[6] * here) * k_row, -1)
        return result - (loss + out) * here

    for sx in range(2):
        @pl.when(jnp.logical_not(has_x[sx]))
        def _(sx=sx):
            (from_lo, from_hi)[sx][...] = jnp.zeros_like(from_lo)
    for sy in range(2):
        @pl.when(jnp.logical_not(has_y[sy]))
        def _(sy=sy):
            col_in[sy] = jnp.zeros_like(col_in[sy])
    for sx, sy in itertools.product((0, 1), (0, 1)):
        @pl.when(jnp.logical_not(has_x[sx] & has_y[sy]))
        def _(sx=sx, sy=sy):
            cor_in[sx, sy] = jnp.zeros_like(cor_in[sx, sy])

    for m in range(M):
        for r in range(CI):
            dpad[m, r + 2, 8 : 8 + CJ] = d_ref[m, r]

    pl.semaphore_wait(known.at[0], len(TOLD[0]))
    tell(1)

    for sy in range(2):
        @pl.when(has_y[sy])
        def _(sy=sy):
            incoming_y(sy).wait_recv()
    for sx, sy in itertools.product((0, 1), (0, 1)):
        @pl.when(has_x[sx] & has_y[sy])
        def _(sx=sx, sy=sy):
            incoming_c(sx, sy).wait_recv()

    for m in range(M):
        for sy, at_col in enumerate((7, 8 + CJ)):
            for r in range(CI):
                dpad[m, r + 2, at_col : at_col + 1] = col_in[sy, m, r : r + 1]
            strip[m, sy, 2 : 2 + CI] = col_in[sy, m, 0:CI]
            for sx, r0 in enumerate((0, CI + 2)):
                strip[m, sy, r0 : r0 + 2] = cor_in[sx, sy, 2 * m : 2 * m + 2]
                for q in range(2):
                    dpad[m, r0 + q, at_col : at_col + 1] = cor_in[sx, sy, 2 * m + q : 2 * m + q + 1]

    inside_hi = (gx < GX - 1).astype(F32)
    for m in range(M):
        c, make_u, make_v, gain_j, loss = coefficients(m)
        for sx in range(2):
            @pl.when(has_x[sx])
            def _(sx=sx, m=m):
                incoming_x(sx, m).wait_recv()
        for q in range(2):
            dpad[m, q, 8 : 8 + CJ] = from_lo[m, 2 + q]
            dpad[m, CI + 2 + q, 8 : 8 + CJ] = from_hi[m, q]

        def full(r):
            if r < 0:
                return from_lo[m, CI + r]
            if r >= CI:
                return from_hi[m, r - CI]
            return d_ref[m, r]

        for r in range(-2, CI + 2):
            u = image(
                c, make_u, make_v, gain_j, loss, row_scalars(c, r),
                full(r - 2), full(r - 1), full(r), full(r + 1), full(r + 2),
                dpad[m, r + 2, 7 : 7 + CJ], dpad[m, r + 2, 9 : 9 + CJ],
            )
            if r >= CI:
                u = u * inside_hi
            upad[m, r + 2, 8 : 8 + CJ] = u

        i4 = (first_i + lax.broadcasted_iota(jnp.int32, (CI, NK), 0)).astype(F32)
        scalars = (
            c[1] * (i4 + 1.0),
            0.5 * c[4] * (i4 + 2.0) * (i4 + 1.0),
            c[1] * i4 + 0.5 * c[4] * i4 * (i4 - 1.0),
        )
        for sy, (jj, at_col) in enumerate(((-1, 7), (CJ, 8 + CJ))):
            j = jnp.full((1, NK), (first_j + jj).astype(F32))
            ratio = j / c[7]
            mu = c[0] / (1.0 + ratio * ratio)
            lo = mu + make_v + c[3] * j + (c[5] + c[6]) * k_row
            inner, outer = col_out[sy, m, 0:CI], col_in[sy, m, CI : 2 * CI]
            left, right = (outer, inner) if sy == 0 else (inner, outer)
            u = image(
                c, mu, make_v, c[3] * (j + 1.0), lo, scalars,
                strip[m, sy, 0:4], strip[m, sy, 1:5], strip[m, sy, 2:6], strip[m, sy, 3:7], strip[m, sy, 4:8],
                left, right,
            )
            if sy == 1:
                u = u * (gy < GY - 1).astype(F32)
            for r in range(CI):
                upad[m, r + 2, at_col : at_col + 1] = u[r : r + 1]

        sums = [jnp.zeros((8, NK), F32) for _ in PAIRS]
        for r in range(CI):
            mid = lambda q: upad[m, q + 2, 8 : 8 + CJ]
            u2 = image(
                c, make_u, make_v, gain_j, loss, row_scalars(c, r),
                mid(r - 2), mid(r - 1), mid(r), mid(r + 1), mid(r + 2),
                upad[m, r + 2, 7 : 7 + CJ], upad[m, r + 2, 9 : 9 + CJ],
            )
            out_ref[m, r] = u2
            basis = (d_ref[m, r], mid(r), u2)
            for p, (a, b) in enumerate(PAIRS):
                product = basis[a] * basis[b]
                sums[p] = sums[p] + product[0:8] + product[8:16]
        for p in range(len(PAIRS)):
            rows[p * M + m : p * M + m + 1] = jnp.sum(sums[p], axis=0, keepdims=True)

    n_rows = len(PAIRS) * M
    column = jnp.sum(rows[...], axis=1, keepdims=True)
    lanes = lax.broadcasted_iota(jnp.int32, (n_rows, NK), 1)
    places = lax.broadcasted_iota(jnp.int32, (n_rows, NK), 0)
    acc = jnp.sum(jnp.where(lanes == places, column, 0.0), axis=0, keepdims=True)

    total[0] = acc

    def early_copy(p):
        return pltpu.make_async_remote_copy(
            src_ref=total.at[0], dst_ref=direct.at[pl.ds((gx - 4 * FAR_Z) * GY + gy, 1)], send_sem=e_send.at[0], recv_sem=e_recv.at[0],
            device_id=p, device_id_type=MESH,
        )

    @pl.when(far)
    def _():
        for p in EARLY:
            early_copy(p).start()

    def y_row(a):
        return pltpu.make_async_remote_copy(
            src_ref=total.at[0], dst_ref=slots_gy.at[pl.ds(gy, 1)], send_sem=r_send.at[0], recv_sem=r_recv.at[0],
            device_id=(gx, lax.rem(gy + a, GY)), device_id_type=MESH,
        )

    def x_row(a):
        return pltpu.make_async_remote_copy(
            src_ref=total.at[1], dst_ref=slots_gx.at[pl.ds(gx, 1)], send_sem=r_send.at[1], recv_sem=r_recv.at[1],
            device_id=(lax.rem(gx + a, GX), gy), device_id_type=MESH,
        )

    def awaited(rows_ref, send_sem, recv_sem):
        return pltpu.make_async_remote_copy(
            src_ref=rows_ref, dst_ref=rows_ref, send_sem=send_sem, recv_sem=recv_sem,
            device_id=(gx, lax.rem(gy + 1, GY)), device_id_type=MESH,
        )

    pl.semaphore_wait(known.at[1], len(TOLD[1]))
    tell(2)
    for a in STAGE_GY:
        y_row(a).start()
    slots_gy[pl.ds(gy, 1)] = acc
    y_rows = awaited(slots_gy.at[0 : GY - 1], r_send.at[0], r_recv.at[0])
    y_rows.wait_recv()
    acc = row_sum(slots_gy[...])
    total[1] = acc
    slots_gx[pl.ds(gx, 1)] = acc

    def wanted(a):
        return jnp.logical_not(far & is_early(lax.rem(gx + a, GX), gy))

    pl.semaphore_wait(known.at[2], len(TOLD[2]))
    for a in STAGE_GX:
        @pl.when(wanted(a))
        def _(a=a):
            x_row(a).start()

    y_rows.wait_send()

    @pl.when(far)
    def _():
        for p in EARLY:
            early_copy(p).wait_send()
        for a in STAGE_GX:
            @pl.when(wanted(a))
            def _(a=a):
                x_row(a).wait_send()

    @pl.when(jnp.logical_not(far))
    def _():
        awaited(slots_gx.at[0 : GX - 1], r_send.at[1], r_recv.at[1]).wait_send()

    for sy in range(2):
        @pl.when(has_y[sy])
        def _(sy=sy):
            y_copy(sy).wait_send()
    for sx, sy in itertools.product((0, 1), (0, 1)):
        @pl.when(has_x[sx] & has_y[sy])
        def _(sx=sx, sy=sy):
            c_copy(sx, sy).wait_send()
    for m in range(M):
        for sx in range(2):
            @pl.when(has_x[sx])
            def _(sx=sx, m=m):
                x_copy(sx, m).wait_send()

    @pl.when(early)
    def _():
        awaited(slots_gx.at[0 : 4 * FAR_Z - 1], r_send.at[1], r_recv.at[1]).wait_recv()
        near_sum = row_sum(slots_gx[0 : 4 * FAR_Z])
        awaited(direct, e_send.at[0], e_recv.at[0]).wait_recv()
        total[2] = near_sum + row_sum(direct[...])

    @pl.when(jnp.logical_not(early))
    def _():
        awaited(slots_gx.at[0 : GX - 1], r_send.at[1], r_recv.at[1]).wait_recv()
        total[2] = row_sum(slots_gx[...])

    acc = total[2]

    picked = [acc if p == 0 else roll_lanes(acc, -M * p) for p in range(len(PAIRS))]
    ok = lane < M
    picked = [jnp.where(ok, value, 1.0) for value in picked]
    scale = 1.0 / picked[0]
    a1, a2, b11, b12, b22 = [value * scale for value in picked[1:]]
    h00 = a1
    n1 = jnp.maximum(b11 - h00 * h00, TINY)
    h10 = jnp.sqrt(n1)
    e = a2 - h00 * a1
    h01 = e / h10
    h11 = ((b12 - h00 * b11) - h00 * e) / n1
    ss = (b22 - h00 * b12) - h00 * (b12 - h00 * b11)
    h21 = jnp.sqrt(jnp.maximum(ss / n1 - h01 * h01 - h11 * h11, TINY))

    step_scale = lam_row * TAU
    entries = [step_scale * h for h in (h00, h10, h01, h11, h21)]
    small = 1.0 / 2.0**SQUARINGS
    g00, g10, g01, g11, g21 = [entry * small for entry in entries]
    one, zero = jnp.ones_like(h00), jnp.zeros_like(h00)
    p00, p01, p10, p11 = one, zero, zero, one
    w0 = w1 = zero
    for term in range(TAYLOR_TERMS, 0, -1):
        f = 1.0 / term
        w0, w1 = g21 * f * p10, g21 * f * p11
        q00 = 1.0 + (g00 * f * p00 + g01 * f * p10)
        q01 = g00 * f * p01 + g01 * f * p11
        q10 = g10 * f * p00 + g11 * f * p10
        q11 = 1.0 + (g10 * f * p01 + g11 * f * p11)
        p00, p01, p10, p11 = q00, q01, q10, q11
    for _ in range(SQUARINGS):
        w0, w1 = w0 + (w0 * p00 + w1 * p10), w1 + (w0 * p01 + w1 * p11)
        q00 = p00 * p00 + p01 * p10
        q01 = p00 * p01 + p01 * p11
        q10 = p10 * p00 + p11 * p10
        q11 = p10 * p01 + p11 * p11
        p00, p01, p10, p11 = q00, q01, q10, q11
    e0, e1, e2 = p00, p10, w0
    inv10 = 1.0 / h10
    e2 = e2 / h21
    f0 = e0 - e1 * h00 * inv10 + e2 * (h11 * h00 * inv10 - h01)
    f1 = (e1 - e2 * (h00 + h11)) * inv10
    f2 = e2 * inv10

    eye = lax.broadcasted_iota(jnp.int32, (8, NK), 0) == lax.broadcasted_iota(jnp.int32, (8, NK), 1)
    lanes8 = lax.broadcasted_iota(jnp.int32, (8, NK), 1)
    table = jnp.zeros((8, NK), F32)
    for q, entry in enumerate(entries):
        column = jnp.sum(jnp.where(eye, entry, 0.0), axis=1, keepdims=True)
        table = jnp.where(lanes8 == q, column, table)
    entry_ref[...] = table[:M, :5]

    for m in range(M):
        s0, s1, s2 = (jnp.broadcast_to(f[:, m : m + 1], (CJ, NK)) for f in (f0, f1, f2))
        for r in range(CI):
            out_ref[m, r] = s0 * d_ref[m, r] + s1 * upad[m, r + 2, 8 : 8 + CJ] + s2 * out_ref[m, r]


def store(field_ref, entry_ref, field_out, entry_out, sems):
    copies = [
        pltpu.make_async_copy(field_ref, field_out, sems.at[0]),
        pltpu.make_async_copy(entry_ref, entry_out, sems.at[1]),
    ]
    for copy in copies:
        copy.start()
    for copy in copies:
        copy.wait()


def shards(density, rate_table):
    vmem = functools.partial(pltpu.VMEM, dtype=F32)
    dma = pltpu.SemaphoreType.DMA
    results = pl.pallas_call(
        kernel,
        out_shape=(pltpu.VMEM(density.shape, F32), pltpu.VMEM((M, 5), F32)),
        in_specs=[pl.BlockSpec(memory_space=pl.ANY), pl.BlockSpec(memory_space=pl.ANY)],
        out_specs=(pl.BlockSpec(memory_space=pltpu.VMEM), pl.BlockSpec(memory_space=pltpu.VMEM)),
        scratch_shapes=[
            vmem((M, CI, CJ, NK)),
            pltpu.SMEM((M, 9), F32),
            vmem((M, CI + 4, 32, NK)),
            vmem((M, CI + 4, 32, NK)),
            vmem((M, CI, CJ, NK)),
            vmem((M, CI, CJ, NK)),
            vmem((2, M, 8, NK)),
            vmem((2, M, 8, NK)),
            vmem((2, 2, 8, NK)),
            vmem((2, 2, 8, NK)),
            vmem((M, 2, 8, NK)),
            vmem((len(PAIRS) * M, NK)),
            vmem((3, 1, NK)),
            vmem((GX, NK)),
            vmem((GY, NK)),
            vmem((N_FAR, NK)),
            dma((2, M)),
            dma((2, M)),
            dma((2,)),
            dma((2,)),
            dma((2, 2)),
            dma((2, 2)),
            dma((2,)),
            dma((2,)),
            dma((1,)),
            dma((1,)),
            dma((2,)),
            pltpu.SemaphoreType.REGULAR((3,)),
        ],
        compiler_params=pltpu.CompilerParams(collective_id=0, has_side_effects=True),
    )(density, rate_table)
    return pl.pallas_call(
        store,
        out_shape=(jax.ShapeDtypeStruct(density.shape, F32), jax.ShapeDtypeStruct((M, 5), F32)),
        in_specs=[pl.BlockSpec(memory_space=pltpu.VMEM)] * 2,
        out_specs=(pl.BlockSpec(memory_space=pl.ANY),) * 2,
        scratch_shapes=[dma((2,))],
        compiler_params=pltpu.CompilerParams(vmem_limit_bytes=1 << 20),
    )(*results)


def solution(mesh):
    specs = (P(None, "gx", "gy", None), P())
    return jax.shard_map(shards, mesh=mesh, in_specs=specs, out_specs=specs, check_vma=False)
```

```python
import functools
import itertools
import math

import jax
import jax.numpy as jnp
from jax import lax
from jax.experimental import pallas as pl
from jax.experimental.pallas import tpu as pltpu
from jax.sharding import PartitionSpec as P

MESH = pl.DeviceIdType.MESH
F32 = jnp.float32
TAU = 0.01
TINY = 1e-36
TAYLOR_TERMS = 16
SQUARINGS = 4
M, CI, CJ, NK = 4, 4, 16, 128
NI, NJ = 128, 256
GX, GY = 32, 16
PAIRS = ((0, 0), (0, 1), (0, 2), (1, 1), (1, 2), (2, 2))


def ring(size):
    return sorted(range(1, size), key=lambda a: -min(a, size - a))


def hops_gx(a):
    z, x = a // 4, a % 4
    return min(z, 8 - z) + min(x, 4 - x)


STAGE_GX = sorted(range(1, GX), key=lambda a: -hops_gx(a))
STAGE_GY = ring(GY)

GREETED = (
    [(0, dx, 0, 0) for dx in (1, 3)]
    + [(0, 0, dy, c) for dy in (1, 7) for c in (1, 0)]
    + [(dz, 0, 0, 0) for dz in (1, 7)]
    + [(0, 0, 0, 1)]
)
TOLD = (
    GREETED,
    [(dz, 0, 0, 0) for dz in (2, 6, 1, 7)] + [(0, 0, dy, 0) for dy in (2, 6)],
    [(dz, 0, 0, 0) for dz in (2, 6)],
)


FAR_Z = 4
N_FAR = (GX - 4 * FAR_Z) * GY
EARLY_REACH = 10


def is_early(gx, gy):
    z, x, y = gx // 4, gx % 4, gy // 2
    return (5 * y + 2 * x + 4 * z <= EARLY_REACH) & (gx + gy > 0)


EARLY = sorted(
    (p for p in itertools.product(range(GX), range(GY)) if is_early(*p)),
    key=lambda p: 5 * (p[1] // 2) + 2 * (p[0] % 4) + 4 * (p[0] // 4),
)
FAR = sorted(
    itertools.product(range(4 * FAR_Z, GX), range(GY)),
    key=lambda p: (abs(p[1] // 2 - 4), abs(p[0] % 4 - 2), p),
)


def row_sum(value):
    return jnp.sum(value, axis=0, keepdims=True)


def roll_lanes(value, shift):
    return pltpu.roll(value, shift % NK, value.ndim - 1)


def kernel(
    d_hbm, rate_hbm, out_ref, entry_ref,
    d_ref, rate_ref, dpad, upad, from_lo, from_hi, col_out, col_in, cor_out, cor_in, strip,
    rows, total, slots_gx, slots_gy, direct,
    x_send, x_recv, y_send, y_recv, c_send, c_recv, r_send, r_recv, e_send, e_recv, load, known,
):
    gx, gy = lax.axis_index("gx"), lax.axis_index("gy")
    z, x, y, core = lax.div(gx, 4), lax.rem(gx, 4), lax.div(gy, 2), lax.rem(gy, 2)
    first_i, first_j = gx * CI, gy * CJ
    has_x = (gx > 0, gx < GX - 1)
    has_y = (gy > 0, gy < GY - 1)
    step = (-1, 1)
    has_edge = ((x == 0) & has_x[0], (x == 3) & has_x[1])

    def at(dx, dy):
        return (gx + dx, gy + dy)

    def offset(dz, dx, dy, dc):
        return (
            lax.rem(z + dz, GX // 4) * 4 + lax.rem(x + dx, 4),
            lax.rem(y + dy, GY // 2) * 2 + lax.rem(core + dc, 2),
        )

    barrier = pltpu.get_barrier_semaphore()
    for o in GREETED[:2]:
        pl.semaphore_signal(barrier, inc=1, device_id=offset(*o), device_id_type=MESH)
    for sx in range(2):
        @pl.when(has_edge[sx])
        def _(sx=sx):
            pl.semaphore_signal(barrier, inc=1, device_id=at(step[sx], 0), device_id_type=MESH)
    for sx, sy in itertools.product((0, 1), (0, 1)):
        @pl.when(has_x[sx] & has_y[sy])
        def _(sx=sx, sy=sy):
            pl.semaphore_signal(barrier, inc=1, device_id=at(step[sx], step[sy]), device_id_type=MESH)
    for o in GREETED[2:]:
        pl.semaphore_signal(barrier, inc=1, device_id=offset(*o), device_id_type=MESH)

    far, early = z >= FAR_Z, is_early(gx, gy)

    @pl.when(early)
    def _():
        for p in FAR:
            pl.semaphore_signal(barrier, inc=1, device_id=p, device_id_type=MESH)

    loads = [
        pltpu.make_async_copy(d_hbm, d_ref, load.at[0]),
        pltpu.make_async_copy(rate_hbm, rate_ref, load.at[1]),
    ]
    for copy in loads:
        copy.start()
    for copy in loads:
        copy.wait()

    for sy, (near, next_near) in enumerate(((0, 1), (CJ - 1, CJ - 2))):
        for m in range(M):
            for r in range(CI):
                col_out[sy, m, r : r + 1] = d_ref[m, r, near : near + 1]
                col_out[sy, m, CI + r : CI + r + 1] = d_ref[m, r, next_near : next_near + 1]
            for sx, r0 in enumerate((0, CI - 2)):
                for q in range(2):
                    cor_out[sx, sy, 2 * m + q : 2 * m + q + 1] = d_ref[m, r0 + q, near : near + 1]

    n_edge = has_edge[0].astype(jnp.int32) + has_edge[1].astype(jnp.int32)
    n_x = has_x[0].astype(jnp.int32) + has_x[1].astype(jnp.int32)
    n_y = has_y[0].astype(jnp.int32) + has_y[1].astype(jnp.int32)
    pl.semaphore_wait(barrier, len(GREETED) + n_edge + n_x * n_y + far.astype(jnp.int32) * len(EARLY))

    def x_copy(sx, m):
        dst = (from_hi, from_lo)[sx]
        return pltpu.make_async_remote_copy(
            src_ref=d_ref.at[m], dst_ref=dst.at[m], send_sem=x_send.at[sx, m], recv_sem=x_recv.at[1 - sx, m],
            device_id=at(step[sx], 0), device_id_type=MESH,
        )

    def y_copy(sy):
        return pltpu.make_async_remote_copy(
            src_ref=col_out.at[sy], dst_ref=col_in.at[1 - sy], send_sem=y_send.at[sy], recv_sem=y_recv.at[1 - sy],
            device_id=at(0, step[sy]), device_id_type=MESH,
        )

    def c_copy(sx, sy):
        return pltpu.make_async_remote_copy(
            src_ref=cor_out.at[sx, sy], dst_ref=cor_in.at[1 - sx, 1 - sy],
            send_sem=c_send.at[sx, sy], recv_sem=c_recv.at[1 - sx, 1 - sy],
            device_id=at(step[sx], step[sy]), device_id_type=MESH,
        )

    def incoming_x(sx, m):
        dst = (from_lo, from_hi)[sx]
        return pltpu.make_async_remote_copy(
            src_ref=d_ref.at[m], dst_ref=dst.at[m], send_sem=x_send.at[sx, m], recv_sem=x_recv.at[sx, m],
            device_id=at(step[sx], 0), device_id_type=MESH,
        )

    def incoming_y(sy):
        return pltpu.make_async_remote_copy(
            src_ref=col_out.at[sy], dst_ref=col_in.at[sy], send_sem=y_send.at[sy], recv_sem=y_recv.at[sy],
            device_id=at(0, step[sy]), device_id_type=MESH,
        )

    def incoming_c(sx, sy):
        return pltpu.make_async_remote_copy(
            src_ref=cor_out.at[sx, sy], dst_ref=cor_in.at[sx, sy],
            send_sem=c_send.at[sx, sy], recv_sem=c_recv.at[sx, sy],
            device_id=at(step[sx], step[sy]), device_id_type=MESH,
        )

    def start_x(m):
        for sx in range(2):
            @pl.when(has_x[sx])
            def _(sx=sx):
                x_copy(sx, m).start()

    start_x(0)
    for sy in range(2):
        @pl.when(has_y[sy])
        def _(sy=sy):
            y_copy(sy).start()
    for sx, sy in itertools.product((0, 1), (0, 1)):
        @pl.when(has_x[sx] & has_y[sy])
        def _(sx=sx, sy=sy):
            c_copy(sx, sy).start()
    for m in range(1, M):
        start_x(m)

    def tell(level):
        for o in TOLD[level]:
            pl.semaphore_signal(known.at[level], inc=1, device_id=offset(*o), device_id_type=MESH)

    tell(0)

    lane = lax.broadcasted_iota(jnp.int32, (1, NK), 1)
    k_row = lane.astype(F32)
    not_first = (lane > 0).astype(F32)
    j_col = (first_j + lax.broadcasted_iota(jnp.int32, (CJ, NK), 0)).astype(F32)
    lam_row = jnp.ones((1, NK), F32)
    rates = []
    for m in range(M):
        c = [rate_ref[m, r] for r in range(9)]
        lam = c[0] + 127.0 * c[1] + c[2] + 255.0 * c[3] + 8001.0 * c[4] + 127.0 * (c[5] + c[6])
        lam_row = jnp.where(lane == m, lam, lam_row)
        rates.append(c)
    inv_row = 1.0 / lam_row

    def coefficients(m):
        inv = inv_row[0, m]
        c = [rates[m][r] * inv for r in range(7)] + rates[m][7:]
        ratio_j = j_col / c[7]
        ratio_k = k_row / c[8]
        make_u = c[0] / (1.0 + ratio_j * ratio_j)
        make_v = c[2] / (1.0 + ratio_k * ratio_k)
        gain_j = c[3] * (j_col + 1.0)
        loss = make_u + make_v + c[3] * j_col + (c[5] + c[6]) * k_row
        return c, make_u, make_v, gain_j, loss

    def row_scalars(c, r):
        i = (first_i + r).astype(F32)
        down = c[1] * (i + 1.0)
        pair = 0.5 * c[4] * (i + 2.0) * (i + 1.0)
        out = c[1] * i + 0.5 * c[4] * i * (i - 1.0)
        return down, pair, out

    def image(c, make_u, make_v, gain_j, loss, scalars, before2, before, here, after, after2, left, right):
        down, pair, out = scalars
        result = make_u * before + down * after + make_v * left + gain_j * right
        result = result + roll_lanes(after2, 1) * (pair * not_first)
        result = result + roll_lanes((c[5] * before2 + c[6] * here) * k_row, -1)
        return result - (loss + out) * here

    for sx in range(2):
        @pl.when(jnp.logical_not(has_x[sx]))
        def _(sx=sx):
            (from_lo, from_hi)[sx][...] = jnp.zeros_like(from_lo)
    for sy in range(2):
        @pl.when(jnp.logical_not(has_y[sy]))
        def _(sy=sy):
            col_in[sy] = jnp.zeros_like(col_in[sy])
    for sx, sy in itertools.product((0, 1), (0, 1)):
        @pl.when(jnp.logical_not(has_x[sx] & has_y[sy]))
        def _(sx=sx, sy=sy):
            cor_in[sx, sy] = jnp.zeros_like(cor_in[sx, sy])

    for m in range(M):
        for r in range(CI):
            dpad[m, r + 2, 8 : 8 + CJ] = d_ref[m, r]

    tables = [coefficients(m) for m in range(M)]
    pl.semaphore_wait(known.at[0], len(TOLD[0]))
    tell(1)

    for sy in range(2):
        @pl.when(has_y[sy])
        def _(sy=sy):
            incoming_y(sy).wait_recv()
    for sx, sy in itertools.product((0, 1), (0, 1)):
        @pl.when(has_x[sx] & has_y[sy])
        def _(sx=sx, sy=sy):
            incoming_c(sx, sy).wait_recv()

    for m in range(M):
        for sy, at_col in enumerate((7, 8 + CJ)):
            for r in range(CI):
                dpad[m, r + 2, at_col : at_col + 1] = col_in[sy, m, r : r + 1]
            strip[m, sy, 2 : 2 + CI] = col_in[sy, m, 0:CI]
            for sx, r0 in enumerate((0, CI + 2)):
                strip[m, sy, r0 : r0 + 2] = cor_in[sx, sy, 2 * m : 2 * m + 2]
                for q in range(2):
                    dpad[m, r0 + q, at_col : at_col + 1] = cor_in[sx, sy, 2 * m + q : 2 * m + q + 1]

    inside_hi = (gx < GX - 1).astype(F32)
    for m in range(M):
        c, make_u, make_v, gain_j, loss = tables[m]
        for sx in range(2):
            @pl.when(has_x[sx])
            def _(sx=sx, m=m):
                incoming_x(sx, m).wait_recv()
        for q in range(2):
            dpad[m, q, 8 : 8 + CJ] = from_lo[m, 2 + q]
            dpad[m, CI + 2 + q, 8 : 8 + CJ] = from_hi[m, q]

        def full(r):
            if r < 0:
                return from_lo[m, CI + r]
            if r >= CI:
                return from_hi[m, r - CI]
            return d_ref[m, r]

        for r in range(-2, CI + 2):
            u = image(
                c, make_u, make_v, gain_j, loss, row_scalars(c, r),
                full(r - 2), full(r - 1), full(r), full(r + 1), full(r + 2),
                dpad[m, r + 2, 7 : 7 + CJ], dpad[m, r + 2, 9 : 9 + CJ],
            )
            if r >= CI:
                u = u * inside_hi
            upad[m, r + 2, 8 : 8 + CJ] = u

        i4 = (first_i + lax.broadcasted_iota(jnp.int32, (CI, NK), 0)).astype(F32)
        scalars = (
            c[1] * (i4 + 1.0),
            0.5 * c[4] * (i4 + 2.0) * (i4 + 1.0),
            c[1] * i4 + 0.5 * c[4] * i4 * (i4 - 1.0),
        )
        for sy, (jj, at_col) in enumerate(((-1, 7), (CJ, 8 + CJ))):
            j = jnp.full((1, NK), (first_j + jj).astype(F32))
            ratio = j / c[7]
            mu = c[0] / (1.0 + ratio * ratio)
            lo = mu + make_v + c[3] * j + (c[5] + c[6]) * k_row
            inner, outer = col_out[sy, m, 0:CI], col_in[sy, m, CI : 2 * CI]
            left, right = (outer, inner) if sy == 0 else (inner, outer)
            u = image(
                c, mu, make_v, c[3] * (j + 1.0), lo, scalars,
                strip[m, sy, 0:4], strip[m, sy, 1:5], strip[m, sy, 2:6], strip[m, sy, 3:7], strip[m, sy, 4:8],
                left, right,
            )
            if sy == 1:
                u = u * (gy < GY - 1).astype(F32)
            for r in range(CI):
                upad[m, r + 2, at_col : at_col + 1] = u[r : r + 1]

        sums = [jnp.zeros((8, NK), F32) for _ in PAIRS]
        for r in range(CI):
            mid = lambda q: upad[m, q + 2, 8 : 8 + CJ]
            u2 = image(
                c, make_u, make_v, gain_j, loss, row_scalars(c, r),
                mid(r - 2), mid(r - 1), mid(r), mid(r + 1), mid(r + 2),
                upad[m, r + 2, 7 : 7 + CJ], upad[m, r + 2, 9 : 9 + CJ],
            )
            out_ref[m, r] = u2
            basis = (d_ref[m, r], mid(r), u2)
            for p, (a, b) in enumerate(PAIRS):
                product = basis[a] * basis[b]
                sums[p] = sums[p] + product[0:8] + product[8:16]
        for p in range(len(PAIRS)):
            rows[p * M + m : p * M + m + 1] = jnp.sum(sums[p], axis=0, keepdims=True)

    n_rows = len(PAIRS) * M
    column = jnp.sum(rows[...], axis=1, keepdims=True)
    lanes = lax.broadcasted_iota(jnp.int32, (n_rows, NK), 1)
    places = lax.broadcasted_iota(jnp.int32, (n_rows, NK), 0)
    acc = jnp.sum(jnp.where(lanes == places, column, 0.0), axis=0, keepdims=True)

    total[0] = acc

    def early_copy(p):
        return pltpu.make_async_remote_copy(
            src_ref=total.at[0], dst_ref=direct.at[pl.ds((gx - 4 * FAR_Z) * GY + gy, 1)], send_sem=e_send.at[0], recv_sem=e_recv.at[0],
            device_id=p, device_id_type=MESH,
        )

    @pl.when(far)
    def _():
        for p in EARLY:
            early_copy(p).start()

    def y_row(a):
        return pltpu.make_async_remote_copy(
            src_ref=total.at[0], dst_ref=slots_gy.at[pl.ds(gy, 1)], send_sem=r_send.at[0], recv_sem=r_recv.at[0],
            device_id=(gx, lax.rem(gy + a, GY)), device_id_type=MESH,
        )

    def x_row(a):
        return pltpu.make_async_remote_copy(
            src_ref=total.at[1], dst_ref=slots_gx.at[pl.ds(gx, 1)], send_sem=r_send.at[1], recv_sem=r_recv.at[1],
            device_id=(lax.rem(gx + a, GX), gy), device_id_type=MESH,
        )

    def awaited(rows_ref, send_sem, recv_sem):
        return pltpu.make_async_remote_copy(
            src_ref=rows_ref, dst_ref=rows_ref, send_sem=send_sem, recv_sem=recv_sem,
            device_id=(gx, lax.rem(gy + 1, GY)), device_id_type=MESH,
        )

    pl.semaphore_wait(known.at[1], len(TOLD[1]))
    tell(2)
    for a in STAGE_GY:
        y_row(a).start()
    slots_gy[pl.ds(gy, 1)] = acc
    y_rows = awaited(slots_gy.at[0 : GY - 1], r_send.at[0], r_recv.at[0])
    y_rows.wait_recv()
    acc = row_sum(slots_gy[...])
    total[1] = acc
    slots_gx[pl.ds(gx, 1)] = acc

    def wanted(a):
        return jnp.logical_not(far & is_early(lax.rem(gx + a, GX), gy))

    pl.semaphore_wait(known.at[2], len(TOLD[2]))
    for a in STAGE_GX:
        @pl.when(wanted(a))
        def _(a=a):
            x_row(a).start()

    y_rows.wait_send()

    @pl.when(far)
    def _():
        for p in EARLY:
            early_copy(p).wait_send()
        for a in STAGE_GX:
            @pl.when(wanted(a))
            def _(a=a):
                x_row(a).wait_send()

    @pl.when(jnp.logical_not(far))
    def _():
        awaited(slots_gx.at[0 : GX - 1], r_send.at[1], r_recv.at[1]).wait_send()

    for sy in range(2):
        @pl.when(has_y[sy])
        def _(sy=sy):
            y_copy(sy).wait_send()
    for sx, sy in itertools.product((0, 1), (0, 1)):
        @pl.when(has_x[sx] & has_y[sy])
        def _(sx=sx, sy=sy):
            c_copy(sx, sy).wait_send()
    for m in range(M):
        for sx in range(2):
            @pl.when(has_x[sx])
            def _(sx=sx, m=m):
                x_copy(sx, m).wait_send()

    @pl.when(early)
    def _():
        awaited(slots_gx.at[0 : 4 * FAR_Z - 1], r_send.at[1], r_recv.at[1]).wait_recv()
        near_sum = row_sum(slots_gx[0 : 4 * FAR_Z])
        awaited(direct, e_send.at[0], e_recv.at[0]).wait_recv()
        total[2] = near_sum + row_sum(direct[...])

    @pl.when(jnp.logical_not(early))
    def _():
        awaited(slots_gx.at[0 : GX - 1], r_send.at[1], r_recv.at[1]).wait_recv()
        total[2] = row_sum(slots_gx[...])

    acc = total[2]

    picked = [acc if p == 0 else roll_lanes(acc, -M * p) for p in range(len(PAIRS))]
    ok = lane < M
    picked = [jnp.where(ok, value, 1.0) for value in picked]
    scale = 1.0 / picked[0]
    a1, a2, b11, b12, b22 = [value * scale for value in picked[1:]]
    h00 = a1
    n1 = jnp.maximum(b11 - h00 * h00, TINY)
    h10 = jnp.sqrt(n1)
    e = a2 - h00 * a1
    h01 = e / h10
    h11 = ((b12 - h00 * b11) - h00 * e) / n1
    ss = (b22 - h00 * b12) - h00 * (b12 - h00 * b11)
    h21 = jnp.sqrt(jnp.maximum(ss / n1 - h01 * h01 - h11 * h11, TINY))

    step_scale = lam_row * TAU
    entries = [step_scale * h for h in (h00, h10, h01, h11, h21)]
    small = 1.0 / 2.0**SQUARINGS
    g00, g10, g01, g11, g21 = [entry * small for entry in entries]

    def times(left, right):
        (l00, l01, l10, l11), (r00, r01, r10, r11) = left, right
        return (
            l00 * r00 + l01 * r10,
            l00 * r01 + l01 * r11,
            l10 * r00 + l11 * r10,
            l10 * r01 + l11 * r11,
        )

    g1 = (g00, g01, g10, g11)
    g2 = times(g1, g1)
    g3, g4 = times(g2, g1), times(g2, g2)
    factors = [1.0 / math.factorial(n) for n in range(1, TAYLOR_TERMS + 1)]
    q = None
    for start in range(TAYLOR_TERMS - 4, -1, -4):
        f = factors[start : start + 4]
        part = [f[1] * a + (f[2] * b + f[3] * c) for a, b, c in zip(g1, g2, g3)]
        part[0], part[3] = part[0] + f[0], part[3] + f[0]
        q = part if q is None else [a + b for a, b in zip(part, times(g4, q))]
    w0, w1 = g21 * q[2], g21 * q[3]
    p00, p01, p10, p11 = times(g1, q)
    p00, p11 = 1.0 + p00, 1.0 + p11
    for _ in range(SQUARINGS):
        w0, w1 = w0 + (w0 * p00 + w1 * p10), w1 + (w0 * p01 + w1 * p11)
        q00 = p00 * p00 + p01 * p10
        q01 = p00 * p01 + p01 * p11
        q10 = p10 * p00 + p11 * p10
        q11 = p10 * p01 + p11 * p11
        p00, p01, p10, p11 = q00, q01, q10, q11
    e0, e1, e2 = p00, p10, w0
    inv10 = 1.0 / h10
    e2 = e2 / h21
    f0 = e0 - e1 * h00 * inv10 + e2 * (h11 * h00 * inv10 - h01)
    f1 = (e1 - e2 * (h00 + h11)) * inv10
    f2 = e2 * inv10

    eye = lax.broadcasted_iota(jnp.int32, (8, NK), 0) == lax.broadcasted_iota(jnp.int32, (8, NK), 1)
    lanes8 = lax.broadcasted_iota(jnp.int32, (8, NK), 1)
    table = jnp.zeros((8, NK), F32)
    for q, entry in enumerate(entries):
        column = jnp.sum(jnp.where(eye, entry, 0.0), axis=1, keepdims=True)
        table = jnp.where(lanes8 == q, column, table)
    entry_ref[...] = table[:M, :5]

    for m in range(M):
        s0, s1, s2 = (jnp.broadcast_to(f[:, m : m + 1], (CJ, NK)) for f in (f0, f1, f2))
        for r in range(CI):
            out_ref[m, r] = s0 * d_ref[m, r] + s1 * upad[m, r + 2, 8 : 8 + CJ] + s2 * out_ref[m, r]


def store(field_ref, entry_ref, field_out, entry_out, sems):
    copies = [
        pltpu.make_async_copy(field_ref, field_out, sems.at[0]),
        pltpu.make_async_copy(entry_ref, entry_out, sems.at[1]),
    ]
    for copy in copies:
        copy.start()
    for copy in copies:
        copy.wait()


def shards(density, rate_table):
    vmem = functools.partial(pltpu.VMEM, dtype=F32)
    dma = pltpu.SemaphoreType.DMA
    results = pl.pallas_call(
        kernel,
        out_shape=(pltpu.VMEM(density.shape, F32), pltpu.VMEM((M, 5), F32)),
        in_specs=[pl.BlockSpec(memory_space=pl.ANY), pl.BlockSpec(memory_space=pl.ANY)],
        out_specs=(pl.BlockSpec(memory_space=pltpu.VMEM), pl.BlockSpec(memory_space=pltpu.VMEM)),
        scratch_shapes=[
            vmem((M, CI, CJ, NK)),
            pltpu.SMEM((M, 9), F32),
            vmem((M, CI + 4, 32, NK)),
            vmem((M, CI + 4, 32, NK)),
            vmem((M, CI, CJ, NK)),
            vmem((M, CI, CJ, NK)),
            vmem((2, M, 8, NK)),
            vmem((2, M, 8, NK)),
            vmem((2, 2, 8, NK)),
            vmem((2, 2, 8, NK)),
            vmem((M, 2, 8, NK)),
            vmem((len(PAIRS) * M, NK)),
            vmem((3, 1, NK)),
            vmem((GX, NK)),
            vmem((GY, NK)),
            vmem((N_FAR, NK)),
            dma((2, M)),
            dma((2, M)),
            dma((2,)),
            dma((2,)),
            dma((2, 2)),
            dma((2, 2)),
            dma((2,)),
            dma((2,)),
            dma((1,)),
            dma((1,)),
            dma((2,)),
            pltpu.SemaphoreType.REGULAR((3,)),
        ],
        compiler_params=pltpu.CompilerParams(collective_id=0, has_side_effects=True),
    )(density, rate_table)
    return pl.pallas_call(
        store,
        out_shape=(jax.ShapeDtypeStruct(density.shape, F32), jax.ShapeDtypeStruct((M, 5), F32)),
        in_specs=[pl.BlockSpec(memory_space=pltpu.VMEM)] * 2,
        out_specs=(pl.BlockSpec(memory_space=pl.ANY),) * 2,
        scratch_shapes=[dma((2,))],
        compiler_params=pltpu.CompilerParams(vmem_limit_bytes=1 << 20),
    )(*results)


def solution(mesh):
    specs = (P(None, "gx", "gy", None), P())
    return jax.shard_map(shards, mesh=mesh, in_specs=specs, out_specs=specs, check_vma=False)
```

```python
import functools
import itertools

import jax
import jax.numpy as jnp
from jax import lax
from jax.experimental import pallas as pl
from jax.experimental.pallas import tpu as pltpu
from jax.sharding import PartitionSpec as P

MESH = pl.DeviceIdType.MESH
F32 = jnp.float32
TAU = 0.01
TINY = 1e-36
TAYLOR_TERMS = 16
SQUARINGS = 4
M, CI, CJ, NK = 4, 4, 16, 128
NI, NJ = 128, 256
GX, GY = 32, 16
PAIRS = ((0, 0), (0, 1), (0, 2), (1, 1), (1, 2), (2, 2))


def ring(size):
    return sorted(range(1, size), key=lambda a: -min(a, size - a))


def hops_gx(a):
    z, x = a // 4, a % 4
    return min(z, 8 - z) + min(x, 4 - x)


STAGE_GX = sorted(range(1, GX), key=lambda a: -hops_gx(a))
STAGE_GY = ring(GY)

GREETED = (
    [(0, dx, 0, 0) for dx in (1, 3)]
    + [(0, 0, dy, c) for dy in (1, 7) for c in (1, 0)]
    + [(dz, 0, 0, 0) for dz in (1, 7)]
    + [(0, 0, 0, 1)]
)
TOLD = (
    GREETED,
    [(dz, 0, 0, 0) for dz in (2, 6, 1, 7)] + [(0, 0, dy, 0) for dy in (2, 6)],
    [(dz, 0, 0, 0) for dz in (2, 6)],
)


FAR_Z = 4
N_FAR = (GX - 4 * FAR_Z) * GY
EARLY_REACH = 10


def is_early(gx, gy):
    z, x, y = gx // 4, gx % 4, gy // 2
    return (5 * y + 2 * x + 4 * z <= EARLY_REACH) & (gx + gy > 0)


EARLY = sorted(
    (p for p in itertools.product(range(GX), range(GY)) if is_early(*p)),
    key=lambda p: 5 * (p[1] // 2) + 2 * (p[0] % 4) + 4 * (p[0] // 4),
)
FAR = sorted(
    itertools.product(range(4 * FAR_Z, GX), range(GY)),
    key=lambda p: (abs(p[1] // 2 - 4), abs(p[0] % 4 - 2), p),
)


def row_sum(value):
    return jnp.sum(value, axis=0, keepdims=True)


def roll_lanes(value, shift):
    return pltpu.roll(value, shift % NK, value.ndim - 1)


def kernel(
    d_hbm, rate_hbm, out_ref, entry_ref,
    d_ref, rate_ref, dpad, upad, from_lo, from_hi, col_out, col_in, cor_out, cor_in, strip,
    rows, total, slots_gx, slots_gy, direct,
    x_send, x_recv, y_send, y_recv, c_send, c_recv, r_send, r_recv, e_send, e_recv, load, known,
):
    gx, gy = lax.axis_index("gx"), lax.axis_index("gy")
    z, x, y, core = lax.div(gx, 4), lax.rem(gx, 4), lax.div(gy, 2), lax.rem(gy, 2)
    first_i, first_j = gx * CI, gy * CJ
    has_x = (gx > 0, gx < GX - 1)
    has_y = (gy > 0, gy < GY - 1)
    step = (-1, 1)
    has_edge = ((x == 0) & has_x[0], (x == 3) & has_x[1])

    def at(dx, dy):
        return (gx + dx, gy + dy)

    def offset(dz, dx, dy, dc):
        return (
            lax.rem(z + dz, GX // 4) * 4 + lax.rem(x + dx, 4),
            lax.rem(y + dy, GY // 2) * 2 + lax.rem(core + dc, 2),
        )

    barrier = pltpu.get_barrier_semaphore()
    for sx, sy in itertools.product((0, 1), (0, 1)):
        @pl.when(has_x[sx] & has_y[sy])
        def _(sx=sx, sy=sy):
            pl.semaphore_signal(barrier, inc=1, device_id=at(step[sx], step[sy]), device_id_type=MESH)
    for o in GREETED[:2]:
        pl.semaphore_signal(barrier, inc=1, device_id=offset(*o), device_id_type=MESH)
    for sx in range(2):
        @pl.when(has_edge[sx])
        def _(sx=sx):
            pl.semaphore_signal(barrier, inc=1, device_id=at(step[sx], 0), device_id_type=MESH)
    for o in GREETED[2:]:
        pl.semaphore_signal(barrier, inc=1, device_id=offset(*o), device_id_type=MESH)

    far, early = z >= FAR_Z, is_early(gx, gy)

    @pl.when(early)
    def _():
        for p in FAR:
            pl.semaphore_signal(barrier, inc=1, device_id=p, device_id_type=MESH)

    loads = [
        pltpu.make_async_copy(d_hbm, d_ref, load.at[0]),
        pltpu.make_async_copy(rate_hbm, rate_ref, load.at[1]),
    ]
    for copy in loads:
        copy.start()
    for copy in loads:
        copy.wait()

    for sy, (near, next_near) in enumerate(((0, 1), (CJ - 1, CJ - 2))):
        for m in range(M):
            for r in range(CI):
                col_out[sy, m, r : r + 1] = d_ref[m, r, near : near + 1]
                col_out[sy, m, CI + r : CI + r + 1] = d_ref[m, r, next_near : next_near + 1]
            for sx, r0 in enumerate((0, CI - 2)):
                for q in range(2):
                    cor_out[sx, sy, 2 * m + q : 2 * m + q + 1] = d_ref[m, r0 + q, near : near + 1]

    n_edge = has_edge[0].astype(jnp.int32) + has_edge[1].astype(jnp.int32)
    n_x = has_x[0].astype(jnp.int32) + has_x[1].astype(jnp.int32)
    n_y = has_y[0].astype(jnp.int32) + has_y[1].astype(jnp.int32)
    pl.semaphore_wait(barrier, len(GREETED) + n_edge + n_x * n_y + far.astype(jnp.int32) * len(EARLY))

    def x_copy(sx, m):
        dst = (from_hi, from_lo)[sx]
        return pltpu.make_async_remote_copy(
            src_ref=d_ref.at[m], dst_ref=dst.at[m], send_sem=x_send.at[sx, m], recv_sem=x_recv.at[1 - sx, m],
            device_id=at(step[sx], 0), device_id_type=MESH,
        )

    def y_copy(sy):
        return pltpu.make_async_remote_copy(
            src_ref=col_out.at[sy], dst_ref=col_in.at[1 - sy], send_sem=y_send.at[sy], recv_sem=y_recv.at[1 - sy],
            device_id=at(0, step[sy]), device_id_type=MESH,
        )

    def c_copy(sx, sy):
        return pltpu.make_async_remote_copy(
            src_ref=cor_out.at[sx, sy], dst_ref=cor_in.at[1 - sx, 1 - sy],
            send_sem=c_send.at[sx, sy], recv_sem=c_recv.at[1 - sx, 1 - sy],
            device_id=at(step[sx], step[sy]), device_id_type=MESH,
        )

    def incoming_x(sx, m):
        dst = (from_lo, from_hi)[sx]
        return pltpu.make_async_remote_copy(
            src_ref=d_ref.at[m], dst_ref=dst.at[m], send_sem=x_send.at[sx, m], recv_sem=x_recv.at[sx, m],
            device_id=at(step[sx], 0), device_id_type=MESH,
        )

    def incoming_y(sy):
        return pltpu.make_async_remote_copy(
            src_ref=col_out.at[sy], dst_ref=col_in.at[sy], send_sem=y_send.at[sy], recv_sem=y_recv.at[sy],
            device_id=at(0, step[sy]), device_id_type=MESH,
        )

    def incoming_c(sx, sy):
        return pltpu.make_async_remote_copy(
            src_ref=cor_out.at[sx, sy], dst_ref=cor_in.at[sx, sy],
            send_sem=c_send.at[sx, sy], recv_sem=c_recv.at[sx, sy],
            device_id=at(step[sx], step[sy]), device_id_type=MESH,
        )

    def start_x(m):
        for sx in range(2):
            @pl.when(has_x[sx])
            def _(sx=sx):
                x_copy(sx, m).start()

    start_x(0)
    for sy in range(2):
        @pl.when(has_y[sy])
        def _(sy=sy):
            y_copy(sy).start()
    for sx, sy in itertools.product((0, 1), (0, 1)):
        @pl.when(has_x[sx] & has_y[sy])
        def _(sx=sx, sy=sy):
            c_copy(sx, sy).start()
    for m in range(1, M):
        start_x(m)

    def tell(level):
        for o in TOLD[level]:
            pl.semaphore_signal(known.at[level], inc=1, device_id=offset(*o), device_id_type=MESH)

    tell(0)

    lane = lax.broadcasted_iota(jnp.int32, (1, NK), 1)
    k_row = lane.astype(F32)
    not_first = (lane > 0).astype(F32)
    j_col = (first_j + lax.broadcasted_iota(jnp.int32, (CJ, NK), 0)).astype(F32)
    lam_row = jnp.ones((1, NK), F32)
    rates = []
    for m in range(M):
        c = [rate_ref[m, r] for r in range(9)]
        lam = c[0] + 127.0 * c[1] + c[2] + 255.0 * c[3] + 8001.0 * c[4] + 127.0 * (c[5] + c[6])
        lam_row = jnp.where(lane == m, lam, lam_row)
        rates.append(c)
    inv_row = 1.0 / lam_row

    def coefficients(m):
        inv = inv_row[0, m]
        c = [rates[m][r] * inv for r in range(7)] + rates[m][7:]
        ratio_j = j_col / c[7]
        ratio_k = k_row / c[8]
        make_u = c[0] / (1.0 + ratio_j * ratio_j)
        make_v = c[2] / (1.0 + ratio_k * ratio_k)
        gain_j = c[3] * (j_col + 1.0)
        loss = make_u + make_v + c[3] * j_col + (c[5] + c[6]) * k_row
        return c, make_u, make_v, gain_j, loss

    def row_scalars(c, r):
        i = (first_i + r).astype(F32)
        down = c[1] * (i + 1.0)
        pair = 0.5 * c[4] * (i + 2.0) * (i + 1.0)
        out = c[1] * i + 0.5 * c[4] * i * (i - 1.0)
        return down, pair, out

    def image(c, make_u, make_v, gain_j, loss, scalars, before2, before, here, after, after2, left, right):
        down, pair, out = scalars
        result = make_u * before + down * after + make_v * left + gain_j * right
        result = result + roll_lanes(after2, 1) * (pair * not_first)
        result = result + roll_lanes((c[5] * before2 + c[6] * here) * k_row, -1)
        return result - (loss + out) * here

    for sx in range(2):
        @pl.when(jnp.logical_not(has_x[sx]))
        def _(sx=sx):
            (from_lo, from_hi)[sx][...] = jnp.zeros_like(from_lo)
    for sy in range(2):
        @pl.when(jnp.logical_not(has_y[sy]))
        def _(sy=sy):
            col_in[sy] = jnp.zeros_like(col_in[sy])
    for sx, sy in itertools.product((0, 1), (0, 1)):
        @pl.when(jnp.logical_not(has_x[sx] & has_y[sy]))
        def _(sx=sx, sy=sy):
            cor_in[sx, sy] = jnp.zeros_like(cor_in[sx, sy])

    for m in range(M):
        for r in range(CI):
            dpad[m, r + 2, 8 : 8 + CJ] = d_ref[m, r]

    pl.semaphore_wait(known.at[0], len(TOLD[0]))
    tell(1)

    for sy in range(2):
        @pl.when(has_y[sy])
        def _(sy=sy):
            incoming_y(sy).wait_recv()
    for sx, sy in itertools.product((0, 1), (0, 1)):
        @pl.when(has_x[sx] & has_y[sy])
        def _(sx=sx, sy=sy):
            incoming_c(sx, sy).wait_recv()

    for m in range(M):
        for sy, at_col in enumerate((7, 8 + CJ)):
            for r in range(CI):
                dpad[m, r + 2, at_col : at_col + 1] = col_in[sy, m, r : r + 1]
            strip[m, sy, 2 : 2 + CI] = col_in[sy, m, 0:CI]
            for sx, r0 in enumerate((0, CI + 2)):
                strip[m, sy, r0 : r0 + 2] = cor_in[sx, sy, 2 * m : 2 * m + 2]
                for q in range(2):
                    dpad[m, r0 + q, at_col : at_col + 1] = cor_in[sx, sy, 2 * m + q : 2 * m + q + 1]

    inside_hi = (gx < GX - 1).astype(F32)
    for m in range(M):
        c, make_u, make_v, gain_j, loss = coefficients(m)
        for sx in range(2):
            @pl.when(has_x[sx])
            def _(sx=sx, m=m):
                incoming_x(sx, m).wait_recv()
        for q in range(2):
            dpad[m, q, 8 : 8 + CJ] = from_lo[m, 2 + q]
            dpad[m, CI + 2 + q, 8 : 8 + CJ] = from_hi[m, q]

        def full(r):
            if r < 0:
                return from_lo[m, CI + r]
            if r >= CI:
                return from_hi[m, r - CI]
            return d_ref[m, r]

        for r in range(-2, CI + 2):
            u = image(
                c, make_u, make_v, gain_j, loss, row_scalars(c, r),
                full(r - 2), full(r - 1), full(r), full(r + 1), full(r + 2),
                dpad[m, r + 2, 7 : 7 + CJ], dpad[m, r + 2, 9 : 9 + CJ],
            )
            if r >= CI:
                u = u * inside_hi
            upad[m, r + 2, 8 : 8 + CJ] = u

        i4 = (first_i + lax.broadcasted_iota(jnp.int32, (CI, NK), 0)).astype(F32)
        scalars = (
            c[1] * (i4 + 1.0),
            0.5 * c[4] * (i4 + 2.0) * (i4 + 1.0),
            c[1] * i4 + 0.5 * c[4] * i4 * (i4 - 1.0),
        )
        for sy, (jj, at_col) in enumerate(((-1, 7), (CJ, 8 + CJ))):
            j = jnp.full((1, NK), (first_j + jj).astype(F32))
            ratio = j / c[7]
            mu = c[0] / (1.0 + ratio * ratio)
            lo = mu + make_v + c[3] * j + (c[5] + c[6]) * k_row
            inner, outer = col_out[sy, m, 0:CI], col_in[sy, m, CI : 2 * CI]
            left, right = (outer, inner) if sy == 0 else (inner, outer)
            u = image(
                c, mu, make_v, c[3] * (j + 1.0), lo, scalars,
                strip[m, sy, 0:4], strip[m, sy, 1:5], strip[m, sy, 2:6], strip[m, sy, 3:7], strip[m, sy, 4:8],
                left, right,
            )
            if sy == 1:
                u = u * (gy < GY - 1).astype(F32)
            for r in range(CI):
                upad[m, r + 2, at_col : at_col + 1] = u[r : r + 1]

        sums = [jnp.zeros((8, NK), F32) for _ in PAIRS]
        for r in range(CI):
            mid = lambda q: upad[m, q + 2, 8 : 8 + CJ]
            u2 = image(
                c, make_u, make_v, gain_j, loss, row_scalars(c, r),
                mid(r - 2), mid(r - 1), mid(r), mid(r + 1), mid(r + 2),
                upad[m, r + 2, 7 : 7 + CJ], upad[m, r + 2, 9 : 9 + CJ],
            )
            out_ref[m, r] = u2
            basis = (d_ref[m, r], mid(r), u2)
            for p, (a, b) in enumerate(PAIRS):
                product = basis[a] * basis[b]
                sums[p] = sums[p] + product[0:8] + product[8:16]
        for p in range(len(PAIRS)):
            rows[p * M + m : p * M + m + 1] = jnp.sum(sums[p], axis=0, keepdims=True)

    n_rows = len(PAIRS) * M
    column = jnp.sum(rows[...], axis=1, keepdims=True)
    lanes = lax.broadcasted_iota(jnp.int32, (n_rows, NK), 1)
    places = lax.broadcasted_iota(jnp.int32, (n_rows, NK), 0)
    acc = jnp.sum(jnp.where(lanes == places, column, 0.0), axis=0, keepdims=True)

    total[0] = acc

    def early_copy(p):
        return pltpu.make_async_remote_copy(
            src_ref=total.at[0], dst_ref=direct.at[pl.ds((gx - 4 * FAR_Z) * GY + gy, 1)], send_sem=e_send.at[0], recv_sem=e_recv.at[0],
            device_id=p, device_id_type=MESH,
        )

    @pl.when(far)
    def _():
        for p in EARLY:
            early_copy(p).start()

    def y_row(a):
        return pltpu.make_async_remote_copy(
            src_ref=total.at[0], dst_ref=slots_gy.at[pl.ds(gy, 1)], send_sem=r_send.at[0], recv_sem=r_recv.at[0],
            device_id=(gx, lax.rem(gy + a, GY)), device_id_type=MESH,
        )

    def x_row(a):
        return pltpu.make_async_remote_copy(
            src_ref=total.at[1], dst_ref=slots_gx.at[pl.ds(gx, 1)], send_sem=r_send.at[1], recv_sem=r_recv.at[1],
            device_id=(lax.rem(gx + a, GX), gy), device_id_type=MESH,
        )

    def awaited(rows_ref, send_sem, recv_sem):
        return pltpu.make_async_remote_copy(
            src_ref=rows_ref, dst_ref=rows_ref, send_sem=send_sem, recv_sem=recv_sem,
            device_id=(gx, lax.rem(gy + 1, GY)), device_id_type=MESH,
        )

    pl.semaphore_wait(known.at[1], len(TOLD[1]))
    tell(2)
    for a in STAGE_GY:
        y_row(a).start()
    slots_gy[pl.ds(gy, 1)] = acc
    y_rows = awaited(slots_gy.at[0 : GY - 1], r_send.at[0], r_recv.at[0])
    y_rows.wait_recv()
    acc = row_sum(slots_gy[...])
    total[1] = acc
    slots_gx[pl.ds(gx, 1)] = acc

    def wanted(a):
        return jnp.logical_not(far & is_early(lax.rem(gx + a, GX), gy))

    pl.semaphore_wait(known.at[2], len(TOLD[2]))
    for a in STAGE_GX:
        @pl.when(wanted(a))
        def _(a=a):
            x_row(a).start()

    y_rows.wait_send()

    @pl.when(far)
    def _():
        for p in EARLY:
            early_copy(p).wait_send()
        for a in STAGE_GX:
            @pl.when(wanted(a))
            def _(a=a):
                x_row(a).wait_send()

    @pl.when(jnp.logical_not(far))
    def _():
        awaited(slots_gx.at[0 : GX - 1], r_send.at[1], r_recv.at[1]).wait_send()

    for sy in range(2):
        @pl.when(has_y[sy])
        def _(sy=sy):
            y_copy(sy).wait_send()
    for sx, sy in itertools.product((0, 1), (0, 1)):
        @pl.when(has_x[sx] & has_y[sy])
        def _(sx=sx, sy=sy):
            c_copy(sx, sy).wait_send()
    for m in range(M):
        for sx in range(2):
            @pl.when(has_x[sx])
            def _(sx=sx, m=m):
                x_copy(sx, m).wait_send()

    @pl.when(early)
    def _():
        awaited(slots_gx.at[0 : 4 * FAR_Z - 1], r_send.at[1], r_recv.at[1]).wait_recv()
        near_sum = row_sum(slots_gx[0 : 4 * FAR_Z])
        awaited(direct, e_send.at[0], e_recv.at[0]).wait_recv()
        total[2] = near_sum + row_sum(direct[...])

    @pl.when(jnp.logical_not(early))
    def _():
        awaited(slots_gx.at[0 : GX - 1], r_send.at[1], r_recv.at[1]).wait_recv()
        total[2] = row_sum(slots_gx[...])

    acc = total[2]

    picked = [acc if p == 0 else roll_lanes(acc, -M * p) for p in range(len(PAIRS))]
    ok = lane < M
    picked = [jnp.where(ok, value, 1.0) for value in picked]
    scale = 1.0 / picked[0]
    a1, a2, b11, b12, b22 = [value * scale for value in picked[1:]]
    h00 = a1
    n1 = jnp.maximum(b11 - h00 * h00, TINY)
    h10 = jnp.sqrt(n1)
    e = a2 - h00 * a1
    h01 = e / h10
    h11 = ((b12 - h00 * b11) - h00 * e) / n1
    ss = (b22 - h00 * b12) - h00 * (b12 - h00 * b11)
    h21 = jnp.sqrt(jnp.maximum(ss / n1 - h01 * h01 - h11 * h11, TINY))

    step_scale = lam_row * TAU
    entries = [step_scale * h for h in (h00, h10, h01, h11, h21)]
    small = 1.0 / 2.0**SQUARINGS
    g00, g10, g01, g11, g21 = [entry * small for entry in entries]
    one, zero = jnp.ones_like(h00), jnp.zeros_like(h00)
    p00, p01, p10, p11 = one, zero, zero, one
    w0 = w1 = zero
    for term in range(TAYLOR_TERMS, 0, -1):
        f = 1.0 / term
        w0, w1 = g21 * f * p10, g21 * f * p11
        q00 = 1.0 + (g00 * f * p00 + g01 * f * p10)
        q01 = g00 * f * p01 + g01 * f * p11
        q10 = g10 * f * p00 + g11 * f * p10
        q11 = 1.0 + (g10 * f * p01 + g11 * f * p11)
        p00, p01, p10, p11 = q00, q01, q10, q11
    for _ in range(SQUARINGS):
        w0, w1 = w0 + (w0 * p00 + w1 * p10), w1 + (w0 * p01 + w1 * p11)
        q00 = p00 * p00 + p01 * p10
        q01 = p00 * p01 + p01 * p11
        q10 = p10 * p00 + p11 * p10
        q11 = p10 * p01 + p11 * p11
        p00, p01, p10, p11 = q00, q01, q10, q11
    e0, e1, e2 = p00, p10, w0
    inv10 = 1.0 / h10
    e2 = e2 / h21
    f0 = e0 - e1 * h00 * inv10 + e2 * (h11 * h00 * inv10 - h01)
    f1 = (e1 - e2 * (h00 + h11)) * inv10
    f2 = e2 * inv10

    eye = lax.broadcasted_iota(jnp.int32, (8, NK), 0) == lax.broadcasted_iota(jnp.int32, (8, NK), 1)
    lanes8 = lax.broadcasted_iota(jnp.int32, (8, NK), 1)
    table = jnp.zeros((8, NK), F32)
    for q, entry in enumerate(entries):
        column = jnp.sum(jnp.where(eye, entry, 0.0), axis=1, keepdims=True)
        table = jnp.where(lanes8 == q, column, table)
    entry_ref[...] = table[:M, :5]

    for m in range(M):
        s0, s1, s2 = (jnp.broadcast_to(f[:, m : m + 1], (CJ, NK)) for f in (f0, f1, f2))
        for r in range(CI):
            out_ref[m, r] = s0 * d_ref[m, r] + s1 * upad[m, r + 2, 8 : 8 + CJ] + s2 * out_ref[m, r]


def store(field_ref, entry_ref, field_out, entry_out, sems):
    copies = [
        pltpu.make_async_copy(field_ref, field_out, sems.at[0]),
        pltpu.make_async_copy(entry_ref, entry_out, sems.at[1]),
    ]
    for copy in copies:
        copy.start()
    for copy in copies:
        copy.wait()


def shards(density, rate_table):
    vmem = functools.partial(pltpu.VMEM, dtype=F32)
    dma = pltpu.SemaphoreType.DMA
    results = pl.pallas_call(
        kernel,
        out_shape=(pltpu.VMEM(density.shape, F32), pltpu.VMEM((M, 5), F32)),
        in_specs=[pl.BlockSpec(memory_space=pl.ANY), pl.BlockSpec(memory_space=pl.ANY)],
        out_specs=(pl.BlockSpec(memory_space=pltpu.VMEM), pl.BlockSpec(memory_space=pltpu.VMEM)),
        scratch_shapes=[
            vmem((M, CI, CJ, NK)),
            pltpu.SMEM((M, 9), F32),
            vmem((M, CI + 4, 32, NK)),
            vmem((M, CI + 4, 32, NK)),
            vmem((M, CI, CJ, NK)),
            vmem((M, CI, CJ, NK)),
            vmem((2, M, 8, NK)),
            vmem((2, M, 8, NK)),
            vmem((2, 2, 8, NK)),
            vmem((2, 2, 8, NK)),
            vmem((M, 2, 8, NK)),
            vmem((len(PAIRS) * M, NK)),
            vmem((3, 1, NK)),
            vmem((GX, NK)),
            vmem((GY, NK)),
            vmem((N_FAR, NK)),
            dma((2, M)),
            dma((2, M)),
            dma((2,)),
            dma((2,)),
            dma((2, 2)),
            dma((2, 2)),
            dma((2,)),
            dma((2,)),
            dma((1,)),
            dma((1,)),
            dma((2,)),
            pltpu.SemaphoreType.REGULAR((3,)),
        ],
        compiler_params=pltpu.CompilerParams(collective_id=0, has_side_effects=True),
    )(density, rate_table)
    return pl.pallas_call(
        store,
        out_shape=(jax.ShapeDtypeStruct(density.shape, F32), jax.ShapeDtypeStruct((M, 5), F32)),
        in_specs=[pl.BlockSpec(memory_space=pltpu.VMEM)] * 2,
        out_specs=(pl.BlockSpec(memory_space=pl.ANY),) * 2,
        scratch_shapes=[dma((2,))],
        compiler_params=pltpu.CompilerParams(vmem_limit_bytes=1 << 20),
    )(*results)


def solution(mesh):
    specs = (P(None, "gx", "gy", None), P())
    return jax.shard_map(shards, mesh=mesh, in_specs=specs, out_specs=specs, check_vma=False)
```
